256 devices in a mesh: grid: 64 (over z, x, core), atoms: 4 (over y).
Axes of the slice: x: 4, y: 4, z: 8, core: 2. Of those that a mesh axis runs over, the one named last changes fastest.
Arguments:
- support_tiles: bfloat16 [16384, 160, 128], P(('grid', 'atoms')), may hold values from -6 to 6
- potential: float32 [4194304], P('grid'), may hold values from -6 to 6
- tile_region: int32 [16384, 1], P(('grid', 'atoms')), may hold values from 0 to 63; in each aligned block of 64 rows (0 to 63, 64 to 127, ...) at most 2 rows name the same one
- tile_block: int32 [16384, 1], P(('grid', 'atoms')), may hold values from 0 to 176
- pair_atoms: int32 [4096, 32], P(('grid', 'atoms')), may hold values from 0 to 4095, as said below
Outputs:
- applied: bfloat16 [16384, 160, 128], P(('grid', 'atoms'))
- margin: float32 [4096, 512], P(('grid', 'atoms'))
- hamiltonian: float32 [4096, 512], P(('grid', 'atoms'))
The draws below stay inside these ranges and needn't reach their ends.
Inputs may be any that keep to these rules, and one draw needn't show every extreme that they name: `tile_region`: in the rows of one device no region is named more than 2 times. `pair_atoms`: each partner of an atom lies in the same block of 16 atoms or in the block just before or after it (atom blocks in order, the last block followed by the first), and is never the atom itself.
All inputs are finite; a program needn't handle non-finite values.
Results may differ from the reference program's by a relative error of at most 0.0055.
Values may be sent and summed in bfloat16 or wider, within the bound.
A program may use at most 128 MiB of HBM per device.

```python
import math
import jax
import jax.numpy as jnp
import numpy as np
from jax import lax

ROWS = 160
COLS = 128
TILE = 20480
SPA = 4
SF_DEV = 64
ATOM_DEV = 16
SF = 16384
ATOMS = 4096
REG = 65536
CAP = 2
PAIRS = 32
N_GRID = 64


def draw_pair_atoms(key, part):
    key = jax.random.fold_in(key, 7)
    picks = jax.random.randint(key, (ATOMS, PAIRS), 0, 3 * ATOM_DEV - 1)
    picks = picks.at[0, 0].set(ATOM_DEV - 1).at[ATOM_DEV, 0].set(0)
    atom_order = jnp.arange(ATOMS)
    home = atom_order % ATOM_DEV
    shifted = picks + (picks >= ATOM_DEV + home[:, None]).astype(jnp.int32)
    first = atom_order // ATOM_DEV * ATOM_DEV - ATOM_DEV
    return jnp.mod(first[:, None] + shifted, ATOMS).astype(jnp.int32)


def touch_ends(result, stream_key, low, high):
    place = [jax.random.randint(jax.random.fold_in(stream_key, axis), (), 0, length) for axis, length in enumerate(result.shape)]
    longest = result.shape.index(max(result.shape))
    next_to = place[:longest] + [(place[longest] + 1) % result.shape[longest]] + place[longest + 1:]
    return result.at[tuple(place)].set(low).at[tuple(next_to)].set(high)


def shard_levels(rng, shape, cuts, smallest, high):
    def one(dim, parts):
        heights = jax.random.uniform(jax.random.fold_in(jax.random.fold_in(rng, 6), dim), (parts,), jnp.float32, smallest / len(cuts), high / len(cuts))
        return jnp.repeat(jnp.exp(heights), shape[dim] // parts).reshape((-1,) + (1,) * (len(shape) - dim - 1))

    level = one(*cuts[0])
    for cut in cuts[1:]:
        level = level * one(*cut)
    return level


def shared_out(stream_key, own, number, rows, number_of, top, most, lean):
    ranking = jax.random.permutation(stream_key, number_of)
    packed, usual = portions_of(number_of, rows * top, most, lean, True), portions_of(number_of, rows * top, most, lean, False)
    places = jnp.arange(number_of)

    def named(sizes, turn):
        used = int((sizes > 0).sum())
        fixed = max(1, used // 4)
        passed = fixed + (places - fixed + turn * (used - fixed)) % max(1, number_of - fixed)
        return jnp.zeros((number_of,), jnp.int32).at[ranking[jnp.where(places < fixed, places, passed)]].set(jnp.asarray(sizes, jnp.int32))

    sizes = jnp.where(number % 4 == 0, named(packed, number // 4), named(usual, number - number // 4 - 1))
    mixed = jax.random.permutation(jax.random.fold_in(own, 3), number_of)
    source_of, receiver = mixed[0:number_of // 2 * 2:2], mixed[1:number_of // 2 * 2:2]
    slack = jnp.minimum(sizes[source_of] - 1, most - sizes[receiver]) // 2
    slack = jnp.where((source_of == ranking[0]) | (receiver == ranking[0]) | (sizes[receiver] == 0), 0, jnp.maximum(slack, 0))
    passed = jax.random.randint(jax.random.fold_in(own, 4), (number_of // 2,), 0, 1 << 20) % (slack + 1)
    sizes = sizes.at[source_of].add(-passed).at[receiver].add(passed)
    items = jnp.searchsorted(jnp.cumsum(sizes), jnp.arange(rows * top), side="right").astype(jnp.int32)
    grid = items.reshape(top, rows).T
    grid = grid[jax.random.permutation(jax.random.fold_in(own, 1), rows)]
    turn = jax.random.randint(jax.random.fold_in(own, 2), (rows, 1), 0, top)
    return jnp.take_along_axis(grid, (jnp.arange(top)[None, :] + turn) % top, axis=1)


def portions_of(number_of, total, most, slope, full):
    portions = [(1 << 20) // math.isqrt(rank ** slope) + 1 for rank in range(1, number_of + 1)]
    largest = most if full else min(most, max(-(-total // number_of), total * portions[0] // sum(portions)))
    least = 1 if total - largest >= number_of - 1 else 0
    given, surplus = [largest] + [least] * (number_of - 1), total - largest - least * (number_of - 1)
    while surplus > 0:
        candidates = [i for i in range(1, number_of) if given[i] < largest] or [i for i in range(1, number_of) if given[i] < most]
        pool, remaining = sum([portions[i] for i in candidates]), surplus
        for i in candidates:
            extra = min(most - given[i], max(1, remaining * portions[i] // pool), surplus)
            given[i] = given[i] + extra
            surplus = surplus - extra
    return np.array(given)


def noise(key, shape, width, limit, shards=(), held_as=jnp.bfloat16):
    drawn = width * jax.random.normal(key, shape, jnp.float32)
    if shards:
        drawn = drawn * shard_levels(key, shape, shards, -0.22, 0.18)
    return jnp.clip(drawn, -limit, limit).astype(held_as)


def setup_inputs(seed: int = 0) -> dict:
    key_of = jax.random.split(jax.random.key(seed), 6)
    support_tiles = noise(key_of[0], (SF, ROWS, COLS), 1.0, 6.0, ((0, 256),))
    potential = noise(key_of[1], (N_GRID * REG,), 1.0, 6.0, ((0, 64),), jnp.float32)
    tile_region_keys = jax.random.split(jax.random.fold_in(key_of[2], 1), SF // SF_DEV)
    tile_region_turns = jax.random.permutation(jax.random.fold_in(key_of[2], 3), SF // SF_DEV)
    tile_region = jax.vmap(lambda own, number: shared_out(jax.random.fold_in(key_of[2], 2), own, number, SF_DEV, N_GRID, 1, CAP, 2))(tile_region_keys, tile_region_turns).reshape((SF, 1))
    tile_block = touch_ends(jax.random.randint(key_of[3], (SF, 1), 0, (REG - TILE) // 256 + 1), jax.random.fold_in(key_of[3], 1), 0, ((REG - TILE) // 256 + 1) - 1).astype(jnp.int32)
    pair_atoms = draw_pair_atoms(jax.random.fold_in(key_of[5], 71), 0)
    return dict(support_tiles=support_tiles, potential=potential, tile_region=tile_region, tile_block=tile_block, pair_atoms=pair_atoms)


def filter_matrix(extent):
    indices = jnp.arange(extent)
    spread = jnp.abs(indices[:, None] - indices[None, :])
    coeffs = jnp.array([-49.0 / 18.0, 1.5, -0.15, 1.0 / 90.0], jnp.float32)
    matrix = jnp.where(spread <= 3, coeffs[jnp.minimum(spread, 3)], jnp.float32(0.0))
    return matrix.astype(jnp.bfloat16)


def kinetic_apply(blocked, windows):
    rows_mat = filter_matrix(ROWS).astype(jnp.float32)
    cols_mat = filter_matrix(COLS).astype(jnp.float32)
    values = blocked.astype(jnp.float32)
    second = jnp.einsum('er,brc->bec', rows_mat, values) + jnp.einsum('brc,cd->brd', values, cols_mat)
    return (-0.5 * second + windows * values).astype(jnp.bfloat16)


def reference(support_tiles, potential, tile_region, tile_block, pair_atoms):
    groups = SF // SF_DEV

    def one_group(bundle):
        group_tiles, group_region, group_block = bundle
        starts = (group_region[:, 0] * REG + group_block[:, 0] * 256).astype(jnp.int32)
        windows = jax.vmap(lambda offset: lax.dynamic_slice(potential, (offset,), (TILE,)))(starts)
        return kinetic_apply(group_tiles, windows.reshape(-1, ROWS, COLS))

    applied = lax.map(one_group, (support_tiles.reshape(groups, SF_DEV, ROWS, COLS),
                                  tile_region.reshape(groups, SF_DEV, 1),
                                  tile_block.reshape(groups, SF_DEV, 1))).reshape(SF, ROWS, COLS)
    basis = support_tiles.reshape(ATOMS, SPA, TILE)
    images = applied.reshape(ATOMS, SPA, TILE)
    scale = float(TILE) ** -0.5

    def one_atom(bundle):
        own_basis, own_image, partners = bundle
        distant = basis[partners].astype(jnp.float32)
        stacked = jnp.stack([own_basis, own_image]).astype(jnp.float32)
        sums = jnp.einsum('ksx,pux->kpsu', stacked, distant) * scale
        return sums.reshape(2, PAIRS * SPA * SPA)

    blocks = lax.map(one_atom, (basis, images, pair_atoms))
    return applied, blocks[:, 0], blocks[:, 1]
```

```python
import heapq

import jax
import jax.numpy as jnp
import numpy as np
from jax import lax
from jax.experimental import pallas as pl
from jax.experimental.pallas import tpu as pltpu
from jax.sharding import PartitionSpec as P

MESH = pl.DeviceIdType.MESH
F32, BF16, I32 = jnp.float32, jnp.bfloat16, jnp.int32
NZ, NX, NY = 8, 4, 4
DEVICES = NZ * NX * 2 * NY
COUNT, ROWS, COLS = 64, 160, 128
ATOMS, PAIRS, SPA = 16, 32, 4
REG_ROWS = 512
UP, DOWN = 96, 80
CUT = 80
SPLIT = 192
SIZE = {"A": SPLIT, "B": REG_ROWS - SPLIT}
BASE = {"A": 0, "B": SPLIT}


def plan():
    axes = {"A": "xz", "B": "zx"}
    length = {"x": NX, "z": NZ}
    free, ready, arrivals, met = {}, [], [], {}
    count = 0

    def push(t, cause, message):
        nonlocal count
        heapq.heappush(ready, (t, count, cause, message))
        count += 1

    def starts(t, cause, part, axis, dz, dx):
        for sign in (1, -1):
            push(t, cause, (part, axis, sign, dz, dx, "full"))

    for part in "AB":
        for axis in axes[part]:
            starts(0.0, None, part, axis, 0, 0)
    while ready:
        best = min(
            range(len(ready)),
            key=lambda i: (max(ready[i][0], free.get(ready[i][3][1:3], 0.0)), ready[i][1]),
        )
        t, _, cause, message = ready.pop(best)
        heapq.heapify(ready)
        part, axis, sign, dz, dx, extent = message
        rows = SIZE[part] if extent == "full" else SIZE[part] // 2
        end = max(t, free.get((axis, sign), 0.0)) + rows
        free[axis, sign] = end
        dz, dx = (dz - sign, dx) if axis == "z" else (dz, dx - sign)
        me, t = len(arrivals), end + 60
        arrivals.append((t, me, (part, axis, sign, dz, dx, extent), cause))
        steps, half = abs(dz if axis == "z" else dx), length[axis] // 2
        if extent == "full":
            push(t, me, (part, axis, sign, dz, dx, "full" if steps < half - 1 else "half"))
        if axis == axes[part][0]:
            key = (part, dz % NZ, dx % NX)
            if extent == "full" or key in met:
                starts(t, me, part, axes[part][1], dz, dx)
            met[key] = me
    return sorted(arrivals)


ORDER = plan()
PLACE = {arrival[1]: i for i, arrival in enumerate(ORDER)}
FOLLOW = {}
for i, arrival in enumerate(ORDER):
    FOLLOW.setdefault(None if arrival[3] is None else PLACE[arrival[3]], []).append(i)
for followers in FOLLOW.values():
    followers.sort(key=lambda i: ORDER[i][1])
WHOLE = {}
for i, arrival in enumerate(ORDER):
    WHOLE[arrival[2][0], arrival[2][3] % NZ] = i
COMPLETE = {}
for key, i in WHOLE.items():
    COMPLETE.setdefault(i, []).append(key)


def banded(rows, cols, shift=0):
    i = lax.broadcasted_iota(I32, (rows, cols), 0) + shift
    j = lax.broadcasted_iota(I32, (rows, cols), 1)
    return spread_values(jnp.abs(i - j))


def spread_values(spread):
    coeffs = np.array([-49.0 / 18.0, 1.5, -0.15, 1.0 / 90.0], np.float32)
    coeffs = -0.5 * coeffs.astype(BF16).astype(np.float32)
    out = jnp.zeros(spread.shape, F32)
    for k in range(4):
        out = jnp.where(spread == k, float(coeffs[k]), out)
    return out.astype(BF16)


def two_bands():
    i = lax.broadcasted_iota(I32, (2 * COLS, 2 * COLS), 0)
    j = lax.broadcasted_iota(I32, (2 * COLS, 2 * COLS), 1)
    return spread_values(jnp.where(i // COLS == j // COLS, jnp.abs(i - j), 9))


def cut(pot, region, block, first, rows):
    tile, shift = lax.shift_right_logical(block, 3) + first // 16, 2 * (block & 7)
    chip, core = lax.shift_right_logical(region, 1), region & 1
    parts = []
    for k in range(rows // 16 + 1):
        raw = pot[chip, core, lax.min(tile + k, REG_ROWS // 16 - 1)].astype(F32)
        parts += [raw[0:8], raw[8:16]]
    odd = shift >= 8
    parts = [jnp.where(odd, parts[k + 1], parts[k]) for k in range(rows // 8 + 1)]
    within = shift & 7
    parts = [pltpu.roll(part, (8 - within) & 7, axis=0) for part in parts]
    stays = lax.broadcasted_iota(I32, (8, COLS), 0) < 8 - within
    return jnp.concatenate([jnp.where(stays, parts[k], parts[k + 1]) for k in range(rows // 8)], axis=0)


def apply_block(x_ref, first_in, rows_in, first_out, rows_out, krow, kcol, pot, meta, line, out, x_to, a_to):
    skip = first_out - first_in

    def body(i, _):
        xs, windows = [], []
        for h in range(2):
            f = 2 * i + h
            xs.append(x_ref[f])
            region, block = meta[0, line, 0, f], meta[1, line, 0, f]
            windows.append(cut(pot, region, block, first_out, rows_out))
        x = jnp.concatenate(xs, axis=1)
        kinetic = jnp.dot(krow[...], x, preferred_element_type=F32)
        kinetic = kinetic + jnp.dot(x[skip : skip + rows_out], kcol[...], preferred_element_type=F32)
        for h in range(2):
            f = 2 * i + h
            values = xs[h].astype(F32)
            local = windows[h] * values[skip : skip + rows_out]
            a = (kinetic[:, COLS * h : COLS * (h + 1)] + local).astype(BF16)
            if out is not None:
                out[f] = a
            a_to[pl.ds(f, rows_out, stride=COUNT), :] = a.astype(F32)
            x_to[pl.ds(f, rows_in, stride=COUNT), :] = values
        return 0

    lax.fori_loop(0, COUNT // 2, body, 0)


def gram(first, last, lhs, rhs):
    def rows(refs, r):
        return jnp.concatenate(
            [
                jnp.concatenate(
                    [ref[pl.ds(pl.multiple_of((r + k - start) * COUNT, COUNT), COUNT), :].astype(BF16) for k in range(2)],
                    axis=1,
                )
                for ref, start in refs
            ],
            axis=0,
        )

    def body(i, total):
        r = first + 2 * i
        return total + lax.dot_general(
            rows(lhs, r), rows(rhs, r), (((1,), (1,)), ((), ())), preferred_element_type=F32
        )

    total = jnp.zeros((COUNT * len(lhs), COUNT * len(rhs)), F32)
    return lax.fori_loop(0, (last - first) // 2, body, total, unroll=2)


def lane_pick(x, lanes):
    return jnp.take_along_axis(x, lanes, axis=1, mode="promise_in_bounds")


def kernel(
    tiles_hbm, own_pot, region, block, pairs,
    applied_hbm, margin, hamiltonian,
    pot, tiles, prev, after, applied, krow, kcol,
    t_rows, a_rows, tp_rows, ap_rows, tn_rows, an_rows,
    meta_v, meta, to_prev, to_next, from_prev, from_next, table, table_after,
    send, recv, sib_send, sib_recv, halo_send, halo_recv, small_send, small_recv, local_sem,
):
    g, y = lax.axis_index("grid"), lax.axis_index("atoms")
    z, x, c = g // 8, (g // 2) % 4, g % 2

    def chip(dz, dx):
        return ((z + dz + NZ) % NZ) * NX + (x + dx + NX) % NX

    def at(position):
        position = (position + DEVICES) % DEVICES
        return (position // NY, position % NY)

    me = g * NY + y
    near = {("z", s): (chip(s, 0) * 2 + c, y) for s in (1, -1)}
    near.update({("x", s): (chip(0, s) * 2 + c, y) for s in (1, -1)})
    sibling = (g + 1 - 2 * c, y)
    later, earlier = at(me + 1), at(me - 1)
    everyone = [*near.values(), sibling, later, earlier]
    barrier = pltpu.get_barrier_semaphore()
    for device in everyone:
        pl.semaphore_signal(barrier, inc=1, device_id=device, device_id_type=MESH)

    def remote(src, dst, s, r, device):
        return pltpu.make_async_remote_copy(src, dst, s, r, device_id=device, device_id_type=MESH)

    tiles_in = pltpu.make_async_copy(tiles_hbm, tiles, local_sem.at[0])
    tiles_in.start()
    pot[chip(0, 0), c] = own_pot[...].astype(BF16).reshape(REG_ROWS // 16, 16, COLS)
    krow[...] = banded(ROWS, ROWS)
    kcol[...] = two_bands()
    pl.semaphore_wait(barrier, len(everyone))

    halos = [
        remote(tiles_hbm.at[:, pl.ds(0, UP)], prev, halo_send.at[0], halo_recv.at[0], later),
        remote(tiles_hbm.at[:, pl.ds(CUT, DOWN)], after, halo_send.at[1], halo_recv.at[1], earlier),
        remote(region, meta_v.at[0], halo_send.at[2], halo_recv.at[2], later),
        remote(block, meta_v.at[1], halo_send.at[3], halo_recv.at[3], later),
        remote(region, meta_v.at[2], halo_send.at[4], halo_recv.at[4], earlier),
        remote(block, meta_v.at[3], halo_send.at[5], halo_recv.at[5], earlier),
    ]

    def slab(part, dz, dx, sign, extent):
        low, rows = BASE[part], SIZE[part]
        if extent == "half":
            rows //= 2
            low += 0 if sign > 0 else rows
        return pot.at[chip(dz, dx), c, pl.ds(low // 16, rows // 16)]

    def forward(i):
        part, axis, sign, dz, dx, extent = ORDER[i][2]
        dz, dx = (dz + sign, dx) if axis == "z" else (dz, dx + sign)
        src = slab(part, dz, dx, sign, extent)
        return remote(src, src, send.at[i], recv.at[i], near[axis, sign])

    def plane(key, core):
        part, dz = key
        return pot.at[pl.ds(((z + dz) % NZ) * NX, NX), core, pl.ds(BASE[part] // 16, SIZE[part] // 16)]

    def hand_over(key):
        j = "AB".index(key[0]) * NZ + key[1]
        return remote(plane(key, c), plane(key, c), sib_send.at[j], sib_recv.at[j], sibling)

    def landed(ref, sem):
        pltpu.make_async_copy(ref, ref, sem).wait()

    for i in FOLLOW[None]:
        forward(i).start()
    for copy in halos:
        copy.start()
    own_meta = [
        pltpu.make_async_copy(region, meta.at[0, 0], local_sem.at[1]),
        pltpu.make_async_copy(block, meta.at[1, 0], local_sem.at[2]),
    ]
    for copy in own_meta:
        copy.start()
    handed = []
    for i in range(len(ORDER)):
        part, axis, sign, dz, dx, extent = ORDER[i][2]
        landed(slab(part, dz, dx, sign, extent), recv.at[i])
        for j in FOLLOW.get(i, []):
            forward(j).start()
        for key in COMPLETE.get(i, []):
            hand_over(key).start()
            handed.append(key)
    for key in handed:
        landed(plane(key, 1 - c), sib_recv.at["AB".index(key[0]) * NZ + key[1]])
    tiles_in.wait()
    for copy in own_meta:
        copy.wait()
    apply_block(
        tiles, 0, ROWS, 0, ROWS, krow, kcol, pot, meta, 0, applied, t_rows, a_rows
    )
    out = pltpu.make_async_copy(applied, applied_hbm, local_sem.at[3])
    out.start()
    for copy in halos:
        copy.wait()
    metas = [pltpu.make_async_copy(meta_v.at[k], meta.at[k % 2, 1 + k // 2], local_sem.at[4 + k]) for k in range(4)]
    for copy in metas:
        copy.start()
    for copy in metas:
        copy.wait()
    apply_block(
        prev, 0, UP, 0, CUT, krow.at[0:CUT, 0:UP], kcol, pot, meta, 1, None, tp_rows, ap_rows
    )
    apply_block(
        after, CUT, DOWN, UP, ROWS - UP, krow.at[UP:ROWS, CUT:ROWS], kcol, pot, meta, 2, None,
        tn_rows, an_rows,
    )
    own = [(t_rows, 0), (a_rows, 0)]
    low = gram(0, CUT, own, [(t_rows, 0), (tp_rows, 0), (ap_rows, 0)])
    mid = gram(CUT, UP, own, [(t_rows, 0), (tp_rows, 0), (tn_rows, CUT)])
    high = gram(UP, ROWS, own, [(t_rows, 0), (tn_rows, CUT), (an_rows, UP)])
    to_prev[...] = low[0:COUNT, COUNT:]
    to_next[...] = high[0:COUNT, COUNT:]
    to_prev[:, 0:COUNT] = low[0:COUNT, COUNT : 2 * COUNT] + mid[0:COUNT, COUNT : 2 * COUNT]
    results = [
        remote(to_prev, from_next, small_send.at[0], small_recv.at[0], earlier),
        remote(to_next, from_prev, small_send.at[1], small_recv.at[1], later),
    ]
    for copy in results:
        copy.start()
    scale = float(ROWS * COLS) ** -0.5
    one, two, three = slice(0, COUNT), slice(COUNT, 2 * COUNT), slice(2 * COUNT, 3 * COUNT)
    table[:, two] = (low[:, one] + mid[:, one] + high[:, one]) * scale
    lanes = lax.broadcasted_iota(I32, (ATOMS, COLS), 1)
    wide = jnp.concatenate([pairs[...]] * (COLS // PAIRS), axis=1)
    first = (me - 1) * ATOMS
    wanted = []
    for k in range(SPA):
        partner = lane_pick(wide, lanes // 16 + 8 * k)
        column = ((partner - first + 2 * DEVICES * ATOMS) % (DEVICES * ATOMS)) * SPA + lanes % SPA
        wanted.append(column)
    for copy in results:
        copy.wait()
    table[:, one] = (low[:, two] + mid[:, two] + from_prev[...].T) * scale
    table_after[...] = jnp.zeros_like(table_after)
    table_after[0:COUNT, one] = (high[0:COUNT, two] + from_next[...].T[0:COUNT]) * scale
    table_after[COUNT : 2 * COUNT, one] = (
        high[COUNT : 2 * COUNT, two] + mid[COUNT : 2 * COUNT, three] + from_next[...].T[COUNT : 2 * COUNT]
    ) * scale
    for k, target in ((0, margin), (1, hamiltonian)):
        for q in range(SPA):
            total = jnp.zeros((ATOMS, COLS), F32)
            for s in range(SPA):
                rows = pl.ds(k * COUNT + s, ATOMS, stride=SPA)
                left, right = table[rows, :], table_after[rows, :]
                column = wanted[q]
                inside = column % COLS
                value = jnp.where(column < COLS, lane_pick(left, inside), lane_pick(right, inside))
                total = jnp.where((lanes // SPA) % SPA == s, value, total)
            target[:, q * COLS : (q + 1) * COLS] = total
    for i in range(len(ORDER)):
        forward(i).wait_send()
    for key in handed:
        hand_over(key).wait_send()
    out.wait()


def shards(support_tiles, potential, tile_region, tile_block, pair_atoms):
    vmem, hbm = pl.BlockSpec(memory_space=pltpu.VMEM), pl.BlockSpec(memory_space=pl.ANY)
    dma = pltpu.SemaphoreType.DMA
    messages = len(ORDER)
    return pl.pallas_call(
        kernel,
        out_shape=(
            jax.ShapeDtypeStruct((COUNT, ROWS, COLS), BF16),
            jax.ShapeDtypeStruct((ATOMS, PAIRS * SPA * SPA), F32),
            jax.ShapeDtypeStruct((ATOMS, PAIRS * SPA * SPA), F32),
        ),
        in_specs=[hbm, vmem, vmem, vmem, vmem],
        out_specs=(hbm, vmem, vmem),
        scratch_shapes=[
            pltpu.VMEM((NZ * NX, 2, REG_ROWS // 16, 16, COLS), BF16),
            pltpu.VMEM((COUNT, ROWS, COLS), BF16),
            pltpu.VMEM((COUNT, UP, COLS), BF16),
            pltpu.VMEM((COUNT, DOWN, COLS), BF16),
            pltpu.VMEM((COUNT, ROWS, COLS), BF16),
            pltpu.VMEM((ROWS, ROWS), BF16),
            pltpu.VMEM((2 * COLS, 2 * COLS), BF16),
            *[pltpu.VMEM((rows * COUNT, COLS), F32) for rows in (ROWS, ROWS, UP, CUT, DOWN, ROWS - UP)],
            pltpu.VMEM((4, 1, COUNT), I32),
            pltpu.SMEM((2, 3, 1, COUNT), I32),
            *[pltpu.VMEM((COUNT, 2 * COUNT), F32) for _ in range(4)],
            pltpu.VMEM((2 * COUNT, COLS), F32),
            pltpu.VMEM((2 * COUNT, COLS), F32),
            dma((messages,)), dma((messages,)), dma((2 * NZ,)), dma((2 * NZ,)),
            dma((6,)), dma((6,)), dma((2,)), dma((2,)), dma((8,)),
        ],
        compiler_params=pltpu.CompilerParams(
            collective_id=0, has_side_effects=True, vmem_limit_bytes=60 * 2**20
        ),
    )(
        support_tiles,
        potential.reshape(REG_ROWS, COLS),
        tile_region.reshape(1, COUNT),
        tile_block.reshape(1, COUNT),
        pair_atoms,
    )


def solution(mesh):
    placed = P(("grid", "atoms"))
    return jax.shard_map(
        shards,
        mesh=mesh,
        in_specs=(placed, P("grid"), placed, placed, placed),
        out_specs=(placed, placed, placed),
        check_vma=False,
    )
```

```python
import heapq

import jax
import jax.numpy as jnp
import numpy as np
from jax import lax
from jax.experimental import pallas as pl
from jax.experimental.pallas import tpu as pltpu
from jax.sharding import PartitionSpec as P

MESH = pl.DeviceIdType.MESH
F32, BF16, I32 = jnp.float32, jnp.bfloat16, jnp.int32
NZ, NX, NY = 8, 4, 4
DEVICES = NZ * NX * 2 * NY
COUNT, ROWS, COLS = 64, 160, 128
ATOMS, PAIRS, SPA = 16, 32, 4
REG_ROWS = 512
UP, DOWN = 96, 80
CUT = 80
SPLIT = 160
CHUNKS, RELAYED = 8, 4
CHUNK = COUNT // CHUNKS
SEND_AT = {4: 0, 5: 0, 6: 4, 7: 8, 0: 14, 1: 20, 2: 26, 3: 32}
RELAY_AT = {4: 14, 5: 20, 6: 26, 7: 32}
SIZE = {"A": SPLIT, "B": REG_ROWS - SPLIT}
BASE = {"A": 0, "B": SPLIT}


def plan():
    axes = {"A": "xz", "B": "zx"}
    length = {"x": NX, "z": NZ}
    free, ready, arrivals, met = {}, [], [], {}
    count = 0

    def push(t, cause, message):
        nonlocal count
        heapq.heappush(ready, (t, count, cause, message))
        count += 1

    def starts(t, cause, part, axis, dz, dx):
        for sign in (1, -1):
            push(t, cause, (part, axis, sign, dz, dx, "full"))

    for part in "AB":
        for axis in axes[part]:
            starts(0.0, None, part, axis, 0, 0)
    while ready:
        best = min(
            range(len(ready)),
            key=lambda i: (max(ready[i][0], free.get(ready[i][3][1:3], 0.0)), ready[i][1]),
        )
        t, _, cause, message = ready.pop(best)
        heapq.heapify(ready)
        part, axis, sign, dz, dx, extent = message
        rows = SIZE[part] if extent == "full" else SIZE[part] // 2
        end = max(t, free.get((axis, sign), 0.0)) + rows
        free[axis, sign] = end
        dz, dx = (dz - sign, dx) if axis == "z" else (dz, dx - sign)
        me, t = len(arrivals), end + 300
        arrivals.append((t, me, (part, axis, sign, dz, dx, extent), cause))
        steps, half = abs(dz if axis == "z" else dx), length[axis] // 2
        if extent == "full":
            push(t, me, (part, axis, sign, dz, dx, "full" if steps < half - 1 else "half"))
        if axis == axes[part][0]:
            key = (part, dz % NZ, dx % NX)
            if extent == "full" or key in met:
                starts(t, me, part, axes[part][1], dz, dx)
            met[key] = me
    return sorted(arrivals)


ORDER = plan()
PLACE = {arrival[1]: i for i, arrival in enumerate(ORDER)}
FOLLOW = {}
for i, arrival in enumerate(ORDER):
    FOLLOW.setdefault(None if arrival[3] is None else PLACE[arrival[3]], []).append(i)
for followers in FOLLOW.values():
    followers.sort(key=lambda i: ORDER[i][1])
WHOLE = {}
for i, arrival in enumerate(ORDER):
    WHOLE[arrival[2][0], arrival[2][3] % NZ] = i
COMPLETE = {}
for key, i in WHOLE.items():
    COMPLETE.setdefault(i, []).append(key)


def banded(rows, cols, shift=0):
    i = lax.broadcasted_iota(I32, (rows, cols), 0) + shift
    j = lax.broadcasted_iota(I32, (rows, cols), 1)
    return spread_values(jnp.abs(i - j))


def spread_values(spread):
    coeffs = np.array([-49.0 / 18.0, 1.5, -0.15, 1.0 / 90.0], np.float32)
    coeffs = -0.5 * coeffs.astype(BF16).astype(np.float32)
    out = jnp.zeros(spread.shape, F32)
    for k in range(4):
        out = jnp.where(spread == k, float(coeffs[k]), out)
    return out.astype(BF16)


def two_bands():
    i = lax.broadcasted_iota(I32, (2 * COLS, 2 * COLS), 0)
    j = lax.broadcasted_iota(I32, (2 * COLS, 2 * COLS), 1)
    return spread_values(jnp.where(i // COLS == j // COLS, jnp.abs(i - j), 9))


def cut(pot, region, block, first, rows):
    tile, shift = lax.shift_right_logical(block, 3) + first // 16, 2 * (block & 7)
    chip, core = lax.shift_right_logical(region, 1), region & 1
    parts = []
    for k in range(rows // 16 + 1):
        raw = pot[chip, core, lax.min(tile + k, REG_ROWS // 16 - 1)].astype(F32)
        parts += [raw[0:8], raw[8:16]]
    odd = shift >= 8
    parts = [jnp.where(odd, parts[k + 1], parts[k]) for k in range(rows // 8 + 1)]
    within = shift & 7
    parts = [pltpu.roll(part, (8 - within) & 7, axis=0) for part in parts]
    stays = lax.broadcasted_iota(I32, (8, COLS), 0) < 8 - within
    return jnp.concatenate([jnp.where(stays, parts[k], parts[k + 1]) for k in range(rows // 8)], axis=0)


def pair_of(x_ref, i):
    return [x_ref[2 * i], x_ref[2 * i + 1]]


def filtered(xs, skip, rows, krow, kcol):
    x = jnp.concatenate(xs, axis=1)
    rows_part = jnp.dot(krow[...], x, preferred_element_type=F32)
    return rows_part + jnp.dot(x[skip : skip + rows], kcol[...], preferred_element_type=F32)


def prepare(x_ref, rows, krow, kcol, kinetic, x_to, first, count):
    def body(i, _):
        xs = pair_of(x_ref, i)
        both = filtered(xs, 0, rows, krow, kcol)
        for h in range(2):
            kinetic[2 * i + h] = both[:, COLS * h : COLS * (h + 1)]
            x_to[pl.ds(2 * i + h, rows, stride=COUNT), :] = xs[h].astype(F32)
        return 0

    lax.fori_loop(first, first + count, body, 0, unroll=2)


def finish(x_ref, rows, pot, meta, line, kinetic, out, a_to):
    def body(f, _):
        local = cut(pot, meta[0, line, 0, f], meta[1, line, 0, f], 0, rows) * x_ref[f].astype(F32)
        a = (kinetic[f] + local).astype(BF16)
        out[f] = a
        a_to[pl.ds(f, rows, stride=COUNT), :] = a.astype(F32)
        return 0

    lax.fori_loop(0, COUNT, body, 0, unroll=2)


def apply_block(x_ref, first_in, rows_in, first_out, rows_out, krow, kcol, pot, meta, line, x_to, a_to):
    skip = first_out - first_in

    def body(i, _):
        xs = pair_of(x_ref, i)
        kinetic = filtered(xs, skip, rows_out, krow, kcol)
        for h in range(2):
            f = 2 * i + h
            window = cut(pot, meta[0, line, 0, f], meta[1, line, 0, f], first_out, rows_out)
            values = xs[h].astype(F32)
            a = kinetic[:, COLS * h : COLS * (h + 1)] + window * values[skip : skip + rows_out]
            a_to[pl.ds(f, rows_out, stride=COUNT), :] = a.astype(BF16).astype(F32)
            x_to[pl.ds(f, rows_in, stride=COUNT), :] = values
        return 0

    lax.fori_loop(0, COUNT // 2, body, 0, unroll=2)


def gram(first, last, lhs, rhs):
    def rows(refs, r):
        return jnp.concatenate(
            [
                jnp.concatenate(
                    [ref[pl.ds(pl.multiple_of((r + k - start) * COUNT, COUNT), COUNT), :].astype(BF16) for k in range(4)],
                    axis=1,
                )
                for ref, start in refs
            ],
            axis=0,
        )

    def body(i, total):
        r = first + 4 * i
        return total + lax.dot_general(
            rows(lhs, r), rows(rhs, r), (((1,), (1,)), ((), ())), preferred_element_type=F32
        )

    total = jnp.zeros((COUNT * len(lhs), COUNT * len(rhs)), F32)
    return lax.fori_loop(0, (last - first) // 4, body, total, unroll=2)


def lane_pick(x, lanes):
    return jnp.take_along_axis(x, lanes, axis=1, mode="promise_in_bounds")


def kernel(
    tiles_hbm, own_pot, region, block, pairs,
    applied_hbm, margin, hamiltonian,
    pot, tiles, prev, after, applied, krow, kcol, kinetic,
    t_rows, a_rows, tp_rows, ap_rows, tn_rows, an_rows,
    meta_v, meta, to_prev, to_next, from_prev, from_next, table, table_after,
    relay,
    send, recv, sib_send, sib_recv, halo_send, halo_recv, relay_send, relay_recv, small_send, small_recv, local_sem,
):
    g, y = lax.axis_index("grid"), lax.axis_index("atoms")
    z, x, c = g // 8, (g // 2) % 4, g % 2

    def chip(dz, dx):
        return ((z + dz + NZ) % NZ) * NX + (x + dx + NX) % NX

    def at(position):
        position = (position + DEVICES) % DEVICES
        return (position // NY, position % NY)

    me = g * NY + y
    near = {("z", s): (chip(s, 0) * 2 + c, y) for s in (1, -1)}
    near.update({("x", s): (chip(0, s) * 2 + c, y) for s in (1, -1)})
    sibling = (g + 1 - 2 * c, y)
    later, earlier = at(me + 1), at(me - 1)
    everyone = [*near.values(), sibling, later, earlier]
    barrier = pltpu.get_barrier_semaphore()
    for device in everyone:
        pl.semaphore_signal(barrier, inc=1, device_id=device, device_id_type=MESH)
    at_low, at_high = y == 0, y == NY - 1
    at_end = jnp.logical_or(at_low, at_high)
    side = 2 * (y // (NY - 1)) - 1
    opposite = (g, NY - 1 - y)
    onward, ward = ((g - side + 64) % 64, y), ((g + side + 64) % 64, y)

    @pl.when(at_end)
    def _():
        for device in (opposite, ward):
            pl.semaphore_signal(barrier, inc=1, device_id=device, device_id_type=MESH)

    def remote(src, dst, s, r, device):
        return pltpu.make_async_remote_copy(src, dst, s, r, device_id=device, device_id_type=MESH)

    tiles_in = pltpu.make_async_copy(tiles_hbm, tiles, local_sem.at[0])
    tiles_in.start()
    pot[chip(0, 0), c] = own_pot[...].astype(BF16).reshape(REG_ROWS // 16, 16, COLS)
    krow[...] = banded(ROWS, ROWS)
    kcol[...] = two_bands()
    @pl.when(at_end)
    def _():
        pl.semaphore_wait(barrier, len(everyone) + 2)

    @pl.when(jnp.logical_not(at_end))
    def _():
        pl.semaphore_wait(barrier, len(everyone))

    halos = [
        remote(region, meta_v.at[0], halo_send.at[2 * CHUNKS], halo_recv.at[2 * CHUNKS], later),
        remote(block, meta_v.at[1], halo_send.at[2 * CHUNKS + 1], halo_recv.at[2 * CHUNKS + 1], later),
        remote(region, meta_v.at[2], halo_send.at[2 * CHUNKS + 2], halo_recv.at[2 * CHUNKS + 2], earlier),
        remote(block, meta_v.at[3], halo_send.at[2 * CHUNKS + 3], halo_recv.at[2 * CHUNKS + 3], earlier),
    ]

    def chunk(k, up):
        some = pl.ds(k * CHUNK, CHUNK)
        if up:
            return remote(
                tiles_hbm.at[some, pl.ds(0, UP)], prev.at[some], halo_send.at[2 * k], halo_recv.at[2 * k], later
            )
        return remote(
            tiles_hbm.at[some, pl.ds(CUT, DOWN)], after.at[some], halo_send.at[2 * k + 1], halo_recv.at[2 * k + 1],
            earlier,
        )

    def slot(k, up):
        return relay.at[k - CHUNKS + RELAYED, :, pl.ds(0, UP if up else DOWN)]

    def detour(k, up):
        some = pl.ds(k * CHUNK, CHUNK)
        src = tiles_hbm.at[some, pl.ds(0, UP) if up else pl.ds(CUT, DOWN)]
        j = k - CHUNKS + RELAYED
        return remote(src, slot(k, up), halo_send.at[2 * k + 1 - up], relay_recv.at[j], opposite)

    def send_on(k, up):
        some = pl.ds(k * CHUNK, CHUNK)
        j = k - CHUNKS + RELAYED
        dst = prev.at[some] if up else after.at[some]
        return remote(slot(k, up), dst, relay_send.at[j], halo_recv.at[2 * k + 1 - up], onward)

    def send_chunk(k):
        if k < CHUNKS - RELAYED:
            chunk(k, 1).start()
            chunk(k, 0).start()
            return
        for up, edge in ((1, at_high), (0, at_low)):

            @pl.when(edge)
            def _():
                detour(k, up).start()

            @pl.when(jnp.logical_not(edge))
            def _():
                chunk(k, up).start()

    def relay_chunk(k):
        for up, edge in ((1, at_low), (0, at_high)):

            @pl.when(edge)
            def _():
                landed(slot(k, up), relay_recv.at[k - CHUNKS + RELAYED])
                send_on(k, up).start()

    def relay_sent(k):
        for up, edge in ((1, at_low), (0, at_high)):

            @pl.when(edge)
            def _():
                send_on(k, up).wait_send()

    def slab(part, dz, dx, sign, extent):
        low, rows = BASE[part], SIZE[part]
        if extent == "half":
            rows //= 2
            low += 0 if sign > 0 else rows
        return pot.at[chip(dz, dx), c, pl.ds(low // 16, rows // 16)]

    def forward(i):
        part, axis, sign, dz, dx, extent = ORDER[i][2]
        dz, dx = (dz + sign, dx) if axis == "z" else (dz, dx + sign)
        src = slab(part, dz, dx, sign, extent)
        return remote(src, src, send.at[i], recv.at[i], near[axis, sign])

    def plane(key, core):
        part, dz = key
        return pot.at[pl.ds(((z + dz) % NZ) * NX, NX), core, pl.ds(BASE[part] // 16, SIZE[part] // 16)]

    def hand_over(key):
        j = "AB".index(key[0]) * NZ + key[1]
        return remote(plane(key, c), plane(key, c), sib_send.at[j], sib_recv.at[j], sibling)

    def landed(ref, sem):
        pltpu.make_async_copy(ref, ref, sem).wait()

    for i in FOLLOW[None]:
        forward(i).start()
    for copy in halos:
        copy.start()
    for k, when in SEND_AT.items():
        if when == 0:
            send_chunk(k)
    own_meta = [
        pltpu.make_async_copy(region, meta.at[0, 0], local_sem.at[1]),
        pltpu.make_async_copy(block, meta.at[1, 0], local_sem.at[2]),
    ]
    for copy in own_meta:
        copy.start()
    handed = []
    done = 0
    for i in range(len(ORDER)):
        part, axis, sign, dz, dx, extent = ORDER[i][2]
        landed(slab(part, dz, dx, sign, extent), recv.at[i])
        for j in FOLLOW.get(i, []):
            forward(j).start()
        for key in COMPLETE.get(i, []):
            hand_over(key).start()
            handed.append(key)
        for k, when in SEND_AT.items():
            if when == i + 1:
                send_chunk(k)
        for k, when in RELAY_AT.items():
            if when == i + 1:
                relay_chunk(k)
        if i == 7:
            tiles_in.wait()
        if i >= 8 and i % 2 == 0 and done < COUNT // 2:
            prepare(tiles, ROWS, krow, kcol, kinetic, t_rows, done, 2)
            done += 2
    for key in handed:
        landed(plane(key, 1 - c), sib_recv.at["AB".index(key[0]) * NZ + key[1]])
    for copy in own_meta:
        copy.wait()
    finish(tiles, ROWS, pot, meta, 0, kinetic, applied, a_rows)
    out = pltpu.make_async_copy(applied, applied_hbm, local_sem.at[3])
    out.start()
    for copy in halos:
        copy.wait()
    for k in range(CHUNKS):
        chunk(k, 1).wait()
        chunk(k, 0).wait()
    metas = [pltpu.make_async_copy(meta_v.at[k], meta.at[k % 2, 1 + k // 2], local_sem.at[4 + k]) for k in range(4)]
    for copy in metas:
        copy.start()
    for copy in metas:
        copy.wait()
    apply_block(
        prev, 0, UP, 0, CUT, krow.at[0:CUT, 0:UP], kcol, pot, meta, 1, tp_rows, ap_rows
    )
    apply_block(
        after, CUT, DOWN, UP, ROWS - UP, krow.at[UP:ROWS, CUT:ROWS], kcol, pot, meta, 2,
        tn_rows, an_rows,
    )
    own = [(t_rows, 0), (a_rows, 0)]
    low = gram(0, CUT, own, [(t_rows, 0), (tp_rows, 0), (ap_rows, 0)])
    mid = gram(CUT, UP, own, [(t_rows, 0), (tp_rows, 0), (tn_rows, CUT)])
    high = gram(UP, ROWS, own, [(t_rows, 0), (tn_rows, CUT), (an_rows, UP)])
    to_prev[...] = low[0:COUNT, COUNT:]
    to_next[...] = high[0:COUNT, COUNT:]
    to_prev[:, 0:COUNT] = low[0:COUNT, COUNT : 2 * COUNT] + mid[0:COUNT, COUNT : 2 * COUNT]
    results = [
        remote(to_prev, from_next, small_send.at[0], small_recv.at[0], earlier),
        remote(to_next, from_prev, small_send.at[1], small_recv.at[1], later),
    ]
    for copy in results:
        copy.start()
    scale = float(ROWS * COLS) ** -0.5
    one, two, three = slice(0, COUNT), slice(COUNT, 2 * COUNT), slice(2 * COUNT, 3 * COUNT)
    table[:, two] = (low[:, one] + mid[:, one] + high[:, one]) * scale
    lanes = lax.broadcasted_iota(I32, (ATOMS, COLS), 1)
    wide = jnp.concatenate([pairs[...]] * (COLS // PAIRS), axis=1)
    first = (me - 1) * ATOMS
    wanted = []
    for k in range(SPA):
        partner = lane_pick(wide, lanes // 16 + 8 * k)
        column = ((partner - first + 2 * DEVICES * ATOMS) % (DEVICES * ATOMS)) * SPA + lanes % SPA
        wanted.append(column)
    for copy in results:
        copy.wait()
    table[:, one] = (low[:, two] + mid[:, two] + from_prev[...].T) * scale
    table_after[...] = jnp.zeros_like(table_after)
    table_after[0:COUNT, one] = (high[0:COUNT, two] + from_next[...].T[0:COUNT]) * scale
    table_after[COUNT : 2 * COUNT, one] = (
        high[COUNT : 2 * COUNT, two] + mid[COUNT : 2 * COUNT, three] + from_next[...].T[COUNT : 2 * COUNT]
    ) * scale
    for k, target in ((0, margin), (1, hamiltonian)):
        for q in range(SPA):
            total = jnp.zeros((ATOMS, COLS), F32)
            for s in range(SPA):
                rows = pl.ds(k * COUNT + s, ATOMS, stride=SPA)
                left, right = table[rows, :], table_after[rows, :]
                column = wanted[q]
                inside = column % COLS
                value = jnp.where(column < COLS, lane_pick(left, inside), lane_pick(right, inside))
                total = jnp.where((lanes // SPA) % SPA == s, value, total)
            target[:, q * COLS : (q + 1) * COLS] = total
    for i in range(len(ORDER)):
        forward(i).wait_send()
    for key in handed:
        hand_over(key).wait_send()
    for k in RELAY_AT:
        relay_sent(k)
    out.wait()


def shards(support_tiles, potential, tile_region, tile_block, pair_atoms):
    vmem, hbm = pl.BlockSpec(memory_space=pltpu.VMEM), pl.BlockSpec(memory_space=pl.ANY)
    dma = pltpu.SemaphoreType.DMA
    messages = len(ORDER)
    return pl.pallas_call(
        kernel,
        out_shape=(
            jax.ShapeDtypeStruct((COUNT, ROWS, COLS), BF16),
            jax.ShapeDtypeStruct((ATOMS, PAIRS * SPA * SPA), F32),
            jax.ShapeDtypeStruct((ATOMS, PAIRS * SPA * SPA), F32),
        ),
        in_specs=[hbm, vmem, vmem, vmem, vmem],
        out_specs=(hbm, vmem, vmem),
        scratch_shapes=[
            pltpu.VMEM((NZ * NX, 2, REG_ROWS // 16, 16, COLS), BF16),
            pltpu.VMEM((COUNT, ROWS, COLS), BF16),
            pltpu.VMEM((COUNT, UP, COLS), BF16),
            pltpu.VMEM((COUNT, DOWN, COLS), BF16),
            pltpu.VMEM((COUNT, ROWS, COLS), BF16),
            pltpu.VMEM((ROWS, ROWS), BF16),
            pltpu.VMEM((2 * COLS, 2 * COLS), BF16),
            pltpu.VMEM((COUNT, ROWS, COLS), F32),
            *[pltpu.VMEM((rows * COUNT, COLS), F32) for rows in (ROWS, ROWS, UP, CUT, DOWN, ROWS - UP)],
            pltpu.VMEM((4, 1, COUNT), I32),
            pltpu.SMEM((2, 3, 1, COUNT), I32),
            *[pltpu.VMEM((COUNT, 2 * COUNT), F32) for _ in range(4)],
            pltpu.VMEM((2 * COUNT, COLS), F32),
            pltpu.VMEM((2 * COUNT, COLS), F32),
            pltpu.VMEM((RELAYED, CHUNK, UP, COLS), BF16),
            dma((messages,)), dma((messages,)), dma((2 * NZ,)), dma((2 * NZ,)),
            dma((2 * CHUNKS + 4,)), dma((2 * CHUNKS + 4,)), dma((RELAYED,)), dma((RELAYED,)), dma((2,)), dma((2,)), dma((8,)),
        ],
        compiler_params=pltpu.CompilerParams(
            collective_id=0, has_side_effects=True, vmem_limit_bytes=60 * 2**20
        ),
    )(
        support_tiles,
        potential.reshape(REG_ROWS, COLS),
        tile_region.reshape(1, COUNT),
        tile_block.reshape(1, COUNT),
        pair_atoms,
    )


def solution(mesh):
    placed = P(("grid", "atoms"))
    return jax.shard_map(
        shards,
        mesh=mesh,
        in_specs=(placed, P("grid"), placed, placed, placed),
        out_specs=(placed, placed, placed),
        check_vma=False,
    )
```

```python
import heapq

import jax
import jax.numpy as jnp
import numpy as np
from jax import lax
from jax.experimental import pallas as pl
from jax.experimental.pallas import tpu as pltpu
from jax.sharding import PartitionSpec as P

MESH = pl.DeviceIdType.MESH
F32, BF16, I32 = jnp.float32, jnp.bfloat16, jnp.int32
NZ, NX, NY = 8, 4, 4
DEVICES = NZ * NX * 2 * NY
COUNT, ROWS, COLS = 64, 160, 128
ATOMS, PAIRS, SPA = 16, 32, 4
REG_ROWS = 512
UP, DOWN = 96, 80
PITCH = 72
CUT = 80
SPLIT = 160
CHUNKS, RELAYED = 8, 4
CHUNK = COUNT // CHUNKS
SEND_AT = {4: 0, 5: 0, 6: 4, 7: 8, 0: 14, 1: 20, 2: 26, 3: 32}
RELAY_AT = {4: 14, 5: 20, 6: 26, 7: 32}
SIZE = {"A": SPLIT, "B": REG_ROWS - SPLIT}
BASE = {"A": 0, "B": SPLIT}


def plan():
    axes = {"A": "xz", "B": "zx"}
    length = {"x": NX, "z": NZ}
    free, ready, arrivals, met = {}, [], [], {}
    count = 0

    def push(t, cause, message):
        nonlocal count
        heapq.heappush(ready, (t, count, cause, message))
        count += 1

    def starts(t, cause, part, axis, dz, dx):
        for sign in (1, -1):
            push(t, cause, (part, axis, sign, dz, dx, "full"))

    for part in "AB":
        for axis in axes[part]:
            starts(0.0, None, part, axis, 0, 0)
    while ready:
        best = min(
            range(len(ready)),
            key=lambda i: (max(ready[i][0], free.get(ready[i][3][1:3], 0.0)), ready[i][1]),
        )
        t, _, cause, message = ready.pop(best)
        heapq.heapify(ready)
        part, axis, sign, dz, dx, extent = message
        rows = SIZE[part] if extent == "full" else SIZE[part] // 2
        end = max(t, free.get((axis, sign), 0.0)) + rows
        free[axis, sign] = end
        dz, dx = (dz - sign, dx) if axis == "z" else (dz, dx - sign)
        me, t = len(arrivals), end + 300
        arrivals.append((t, me, (part, axis, sign, dz, dx, extent), cause))
        steps, half = abs(dz if axis == "z" else dx), length[axis] // 2
        if extent == "full":
            push(t, me, (part, axis, sign, dz, dx, "full" if steps < half - 1 else "half"))
        if axis == axes[part][0]:
            key = (part, dz % NZ, dx % NX)
            if extent == "full" or key in met:
                starts(t, me, part, axes[part][1], dz, dx)
            met[key] = me
    return sorted(arrivals)


ORDER = plan()
PLACE = {arrival[1]: i for i, arrival in enumerate(ORDER)}
FOLLOW = {}
for i, arrival in enumerate(ORDER):
    FOLLOW.setdefault(None if arrival[3] is None else PLACE[arrival[3]], []).append(i)
for followers in FOLLOW.values():
    followers.sort(key=lambda i: ORDER[i][1])
WHOLE = {}
for i, arrival in enumerate(ORDER):
    WHOLE[arrival[2][0], arrival[2][3] % NZ] = i
COMPLETE = {}
for key, i in WHOLE.items():
    COMPLETE.setdefault(i, []).append(key)


def banded(rows, cols, shift=0):
    i = lax.broadcasted_iota(I32, (rows, cols), 0) + shift
    j = lax.broadcasted_iota(I32, (rows, cols), 1)
    return spread_values(jnp.abs(i - j))


def spread_values(spread):
    coeffs = np.array([-49.0 / 18.0, 1.5, -0.15, 1.0 / 90.0], np.float32)
    coeffs = -0.5 * coeffs.astype(BF16).astype(np.float32)
    out = jnp.zeros(spread.shape, F32)
    for k in range(4):
        out = jnp.where(spread == k, float(coeffs[k]), out)
    return out.astype(BF16)


def two_bands():
    i = lax.broadcasted_iota(I32, (2 * COLS, 2 * COLS), 0)
    j = lax.broadcasted_iota(I32, (2 * COLS, 2 * COLS), 1)
    return spread_values(jnp.where(i // COLS == j // COLS, jnp.abs(i - j), 9))


def cut(pot, region, block, first, rows):
    tile, shift = lax.shift_right_logical(block, 3) + first // 16, 2 * (block & 7)
    chip, core = lax.shift_right_logical(region, 1), region & 1
    parts = []
    for k in range(rows // 16 + 1):
        raw = pot[chip, core, lax.min(tile + k, REG_ROWS // 16 - 1)].astype(F32)
        parts += [raw[0:8], raw[8:16]]
    odd = shift >= 8
    parts = [jnp.where(odd, parts[k + 1], parts[k]) for k in range(rows // 8 + 1)]
    within = shift & 7
    parts = [pltpu.roll(part, (8 - within) & 7, axis=0) for part in parts]
    stays = lax.broadcasted_iota(I32, (8, COLS), 0) < 8 - within
    return jnp.concatenate([jnp.where(stays, parts[k], parts[k + 1]) for k in range(rows // 8)], axis=0)


def pair_of(x_ref, i):
    return [x_ref[2 * i], x_ref[2 * i + 1]]


def filtered(xs, skip, rows, krow, kcol):
    x = jnp.concatenate(xs, axis=1)
    rows_part = jnp.dot(krow[...], x, preferred_element_type=F32)
    return rows_part + jnp.dot(x[skip : skip + rows], kcol[...], preferred_element_type=F32)


def prepare(x_ref, rows, krow, kcol, kinetic, x_to, first, count):
    def body(i, _):
        xs = pair_of(x_ref, i)
        both = filtered(xs, 0, rows, krow, kcol)
        for h in range(2):
            kinetic[2 * i + h] = both[:, COLS * h : COLS * (h + 1)]
            x_to[pl.ds(2 * i + h, rows, stride=PITCH), :] = xs[h].astype(F32)
        return 0

    lax.fori_loop(first, first + count, body, 0, unroll=2)


def finish(x_ref, rows, pot, meta, line, kinetic, out, a_to):
    def body(f, _):
        local = cut(pot, meta[0, line, 0, f], meta[1, line, 0, f], 0, rows) * x_ref[f].astype(F32)
        a = (kinetic[f] + local).astype(BF16)
        out[f] = a
        a_to[pl.ds(f, rows, stride=PITCH), :] = a.astype(F32)
        return 0

    lax.fori_loop(0, COUNT, body, 0, unroll=2)


def apply_block(x_ref, first_in, rows_in, first_out, rows_out, krow, kcol, pot, meta, line, x_to, a_to):
    skip = first_out - first_in

    def body(i, _):
        xs = pair_of(x_ref, i)
        kinetic = filtered(xs, skip, rows_out, krow, kcol)
        for h in range(2):
            f = 2 * i + h
            window = cut(pot, meta[0, line, 0, f], meta[1, line, 0, f], first_out, rows_out)
            values = xs[h].astype(F32)
            a = kinetic[:, COLS * h : COLS * (h + 1)] + window * values[skip : skip + rows_out]
            a_to[pl.ds(f, rows_out, stride=PITCH), :] = a.astype(BF16).astype(F32)
            x_to[pl.ds(f, rows_in, stride=PITCH), :] = values
        return 0

    lax.fori_loop(0, COUNT // 2, body, 0, unroll=8)


def gram(first, last, lhs, rhs):
    def rows(refs, r):
        return jnp.concatenate(
            [
                jnp.concatenate(
                    [ref[pl.ds(pl.multiple_of((r + k - start) * PITCH, 8), COUNT), :].astype(BF16) for k in range(16)],
                    axis=1,
                )
                for ref, start in refs
            ],
            axis=0,
        )

    def body(i, total):
        r = first + 16 * i
        return total + lax.dot_general(
            rows(lhs, r), rows(rhs, r), (((1,), (1,)), ((), ())), preferred_element_type=F32
        )

    total = jnp.zeros((COUNT * len(lhs), COUNT * len(rhs)), F32)
    return lax.fori_loop(0, (last - first) // 16, body, total, unroll=4)


def lane_pick(x, lanes):
    return jnp.take_along_axis(x, lanes, axis=1, mode="promise_in_bounds")


def kernel(
    tiles_hbm, own_pot, region, block, pairs,
    applied_hbm, margin, hamiltonian,
    pot, tiles, prev, after, applied, krow, kcol, kinetic,
    t_rows, a_rows, tp_rows, ap_rows, tn_rows, an_rows,
    meta_v, meta, to_prev, to_next, from_prev, from_next, table, table_after,
    relay,
    send, recv, sib_send, sib_recv, halo_send, halo_recv, relay_send, relay_recv, small_send, small_recv, local_sem,
):
    g, y = lax.axis_index("grid"), lax.axis_index("atoms")
    z, x, c = g // 8, (g // 2) % 4, g % 2

    def chip(dz, dx):
        return ((z + dz + NZ) % NZ) * NX + (x + dx + NX) % NX

    def at(position):
        position = (position + DEVICES) % DEVICES
        return (position // NY, position % NY)

    me = g * NY + y
    near = {("z", s): (chip(s, 0) * 2 + c, y) for s in (1, -1)}
    near.update({("x", s): (chip(0, s) * 2 + c, y) for s in (1, -1)})
    sibling = (g + 1 - 2 * c, y)
    later, earlier = at(me + 1), at(me - 1)
    everyone = [*near.values(), sibling, later, earlier]
    barrier = pltpu.get_barrier_semaphore()
    for device in everyone:
        pl.semaphore_signal(barrier, inc=1, device_id=device, device_id_type=MESH)
    at_low, at_high = y == 0, y == NY - 1
    at_end = jnp.logical_or(at_low, at_high)
    side = 2 * (y // (NY - 1)) - 1
    opposite = (g, NY - 1 - y)
    onward, ward = ((g - side + 64) % 64, y), ((g + side + 64) % 64, y)

    @pl.when(at_end)
    def _():
        for device in (opposite, ward):
            pl.semaphore_signal(barrier, inc=1, device_id=device, device_id_type=MESH)

    def remote(src, dst, s, r, device):
        return pltpu.make_async_remote_copy(src, dst, s, r, device_id=device, device_id_type=MESH)

    tiles_in = pltpu.make_async_copy(tiles_hbm, tiles, local_sem.at[0])
    tiles_in.start()
    pot[chip(0, 0), c] = own_pot[...].astype(BF16).reshape(REG_ROWS // 16, 16, COLS)
    krow[...] = banded(ROWS, ROWS)
    kcol[...] = two_bands()
    @pl.when(at_end)
    def _():
        pl.semaphore_wait(barrier, len(everyone) + 2)

    @pl.when(jnp.logical_not(at_end))
    def _():
        pl.semaphore_wait(barrier, len(everyone))

    halos = [
        remote(region, meta_v.at[0], halo_send.at[2 * CHUNKS], halo_recv.at[2 * CHUNKS], later),
        remote(block, meta_v.at[1], halo_send.at[2 * CHUNKS + 1], halo_recv.at[2 * CHUNKS + 1], later),
        remote(region, meta_v.at[2], halo_send.at[2 * CHUNKS + 2], halo_recv.at[2 * CHUNKS + 2], earlier),
        remote(block, meta_v.at[3], halo_send.at[2 * CHUNKS + 3], halo_recv.at[2 * CHUNKS + 3], earlier),
    ]

    def chunk(k, up):
        some = pl.ds(k * CHUNK, CHUNK)
        if up:
            return remote(
                tiles_hbm.at[some, pl.ds(0, UP)], prev.at[some], halo_send.at[2 * k], halo_recv.at[2 * k], later
            )
        return remote(
            tiles_hbm.at[some, pl.ds(CUT, DOWN)], after.at[some], halo_send.at[2 * k + 1], halo_recv.at[2 * k + 1],
            earlier,
        )

    def slot(k, up):
        return relay.at[k - CHUNKS + RELAYED, :, pl.ds(0, UP if up else DOWN)]

    def detour(k, up):
        some = pl.ds(k * CHUNK, CHUNK)
        src = tiles_hbm.at[some, pl.ds(0, UP) if up else pl.ds(CUT, DOWN)]
        j = k - CHUNKS + RELAYED
        return remote(src, slot(k, up), halo_send.at[2 * k + 1 - up], relay_recv.at[j], opposite)

    def send_on(k, up):
        some = pl.ds(k * CHUNK, CHUNK)
        j = k - CHUNKS + RELAYED
        dst = prev.at[some] if up else after.at[some]
        return remote(slot(k, up), dst, relay_send.at[j], halo_recv.at[2 * k + 1 - up], onward)

    def send_chunk(k):
        if k < CHUNKS - RELAYED:
            chunk(k, 1).start()
            chunk(k, 0).start()
            return
        for up, edge in ((1, at_high), (0, at_low)):

            @pl.when(edge)
            def _():
                detour(k, up).start()

            @pl.when(jnp.logical_not(edge))
            def _():
                chunk(k, up).start()

    def relay_chunk(k):
        for up, edge in ((1, at_low), (0, at_high)):

            @pl.when(edge)
            def _():
                landed(slot(k, up), relay_recv.at[k - CHUNKS + RELAYED])
                send_on(k, up).start()

    def relay_sent(k):
        for up, edge in ((1, at_low), (0, at_high)):

            @pl.when(edge)
            def _():
                send_on(k, up).wait_send()

    def slab(part, dz, dx, sign, extent):
        low, rows = BASE[part], SIZE[part]
        if extent == "half":
            rows //= 2
            low += 0 if sign > 0 else rows
        return pot.at[chip(dz, dx), c, pl.ds(low // 16, rows // 16)]

    def forward(i):
        part, axis, sign, dz, dx, extent = ORDER[i][2]
        dz, dx = (dz + sign, dx) if axis == "z" else (dz, dx + sign)
        src = slab(part, dz, dx, sign, extent)
        return remote(src, src, send.at[i], recv.at[i], near[axis, sign])

    def plane(key, core):
        part, dz = key
        return pot.at[pl.ds(((z + dz) % NZ) * NX, NX), core, pl.ds(BASE[part] // 16, SIZE[part] // 16)]

    def hand_over(key):
        j = "AB".index(key[0]) * NZ + key[1]
        return remote(plane(key, c), plane(key, c), sib_send.at[j], sib_recv.at[j], sibling)

    def landed(ref, sem):
        pltpu.make_async_copy(ref, ref, sem).wait()

    for i in FOLLOW[None]:
        forward(i).start()
    for copy in halos:
        copy.start()
    for k, when in SEND_AT.items():
        if when == 0:
            send_chunk(k)
    own_meta = [
        pltpu.make_async_copy(region, meta.at[0, 0], local_sem.at[1]),
        pltpu.make_async_copy(block, meta.at[1, 0], local_sem.at[2]),
    ]
    for copy in own_meta:
        copy.start()
    handed = []
    done = 0
    for i in range(len(ORDER)):
        part, axis, sign, dz, dx, extent = ORDER[i][2]
        landed(slab(part, dz, dx, sign, extent), recv.at[i])
        for j in FOLLOW.get(i, []):
            forward(j).start()
        for key in COMPLETE.get(i, []):
            hand_over(key).start()
            handed.append(key)
        for k, when in SEND_AT.items():
            if when == i + 1:
                send_chunk(k)
        for k, when in RELAY_AT.items():
            if when == i + 1:
                relay_chunk(k)
        if i == 7:
            tiles_in.wait()
        if i >= 8 and i % 2 == 0 and done < COUNT // 2:
            prepare(tiles, ROWS, krow, kcol, kinetic, t_rows, done, 2)
            done += 2
    for key in handed:
        landed(plane(key, 1 - c), sib_recv.at["AB".index(key[0]) * NZ + key[1]])
    for copy in own_meta:
        copy.wait()
    finish(tiles, ROWS, pot, meta, 0, kinetic, applied, a_rows)
    out = pltpu.make_async_copy(applied, applied_hbm, local_sem.at[3])
    out.start()
    for copy in halos:
        copy.wait()
    for k in range(CHUNKS):
        chunk(k, 1).wait()
        chunk(k, 0).wait()
    metas = [pltpu.make_async_copy(meta_v.at[k], meta.at[k % 2, 1 + k // 2], local_sem.at[4 + k]) for k in range(4)]
    for copy in metas:
        copy.start()
    for copy in metas:
        copy.wait()
    apply_block(
        prev, 0, UP, 0, CUT, krow.at[0:CUT, 0:UP], kcol, pot, meta, 1, tp_rows, ap_rows
    )
    apply_block(
        after, CUT, DOWN, UP, ROWS - UP, krow.at[UP:ROWS, CUT:ROWS], kcol, pot, meta, 2,
        tn_rows, an_rows,
    )
    own = [(t_rows, 0), (a_rows, 0)]
    low = gram(0, CUT, own, [(t_rows, 0), (tp_rows, 0), (ap_rows, 0)])
    mid = gram(CUT, UP, own, [(t_rows, 0), (tp_rows, 0), (tn_rows, CUT)])
    high = gram(UP, ROWS, own, [(t_rows, 0), (tn_rows, CUT), (an_rows, UP)])
    to_prev[...] = low[0:COUNT, COUNT:]
    to_next[...] = high[0:COUNT, COUNT:]
    to_prev[:, 0:COUNT] = low[0:COUNT, COUNT : 2 * COUNT] + mid[0:COUNT, COUNT : 2 * COUNT]
    results = [
        remote(to_prev, from_next, small_send.at[0], small_recv.at[0], earlier),
        remote(to_next, from_prev, small_send.at[1], small_recv.at[1], later),
    ]
    for copy in results:
        copy.start()
    scale = float(ROWS * COLS) ** -0.5
    one, two, three = slice(0, COUNT), slice(COUNT, 2 * COUNT), slice(2 * COUNT, 3 * COUNT)
    table[:, two] = (low[:, one] + mid[:, one] + high[:, one]) * scale
    lanes = lax.broadcasted_iota(I32, (ATOMS, COLS), 1)
    wide = jnp.concatenate([pairs[...]] * (COLS // PAIRS), axis=1)
    first = (me - 1) * ATOMS
    wanted = []
    for k in range(SPA):
        partner = lane_pick(wide, lanes // 16 + 8 * k)
        column = ((partner - first + 2 * DEVICES * ATOMS) % (DEVICES * ATOMS)) * SPA + lanes % SPA
        wanted.append(column)
    for copy in results:
        copy.wait()
    table[:, one] = (low[:, two] + mid[:, two] + from_prev[...].T) * scale
    table_after[...] = jnp.zeros_like(table_after)
    table_after[0:COUNT, one] = (high[0:COUNT, two] + from_next[...].T[0:COUNT]) * scale
    table_after[COUNT : 2 * COUNT, one] = (
        high[COUNT : 2 * COUNT, two] + mid[COUNT : 2 * COUNT, three] + from_next[...].T[COUNT : 2 * COUNT]
    ) * scale
    for k, target in ((0, margin), (1, hamiltonian)):
        for q in range(SPA):
            total = jnp.zeros((ATOMS, COLS), F32)
            for s in range(SPA):
                rows = pl.ds(k * COUNT + s, ATOMS, stride=SPA)
                left, right = table[rows, :], table_after[rows, :]
                column = wanted[q]
                inside = column % COLS
                value = jnp.where(column < COLS, lane_pick(left, inside), lane_pick(right, inside))
                total = jnp.where((lanes // SPA) % SPA == s, value, total)
            target[:, q * COLS : (q + 1) * COLS] = total
    for i in range(len(ORDER)):
        forward(i).wait_send()
    for key in handed:
        hand_over(key).wait_send()
    for k in RELAY_AT:
        relay_sent(k)
    out.wait()


def shards(support_tiles, potential, tile_region, tile_block, pair_atoms):
    vmem, hbm = pl.BlockSpec(memory_space=pltpu.VMEM), pl.BlockSpec(memory_space=pl.ANY)
    dma = pltpu.SemaphoreType.DMA
    messages = len(ORDER)
    return pl.pallas_call(
        kernel,
        out_shape=(
            jax.ShapeDtypeStruct((COUNT, ROWS, COLS), BF16),
            jax.ShapeDtypeStruct((ATOMS, PAIRS * SPA * SPA), F32),
            jax.ShapeDtypeStruct((ATOMS, PAIRS * SPA * SPA), F32),
        ),
        in_specs=[hbm, vmem, vmem, vmem, vmem],
        out_specs=(hbm, vmem, vmem),
        scratch_shapes=[
            pltpu.VMEM((NZ * NX, 2, REG_ROWS // 16, 16, COLS), BF16),
            pltpu.VMEM((COUNT, ROWS, COLS), BF16),
            pltpu.VMEM((COUNT, UP, COLS), BF16),
            pltpu.VMEM((COUNT, DOWN, COLS), BF16),
            pltpu.VMEM((COUNT, ROWS, COLS), BF16),
            pltpu.VMEM((ROWS, ROWS), BF16),
            pltpu.VMEM((2 * COLS, 2 * COLS), BF16),
            pltpu.VMEM((COUNT, ROWS, COLS), F32),
            *[pltpu.VMEM((rows * PITCH, COLS), F32) for rows in (ROWS, ROWS, UP, CUT, DOWN, ROWS - UP)],
            pltpu.VMEM((4, 1, COUNT), I32),
            pltpu.SMEM((2, 3, 1, COUNT), I32),
            *[pltpu.VMEM((COUNT, 2 * COUNT), F32) for _ in range(4)],
            pltpu.VMEM((2 * COUNT, COLS), F32),
            pltpu.VMEM((2 * COUNT, COLS), F32),
            pltpu.VMEM((RELAYED, CHUNK, UP, COLS), BF16),
            dma((messages,)), dma((messages,)), dma((2 * NZ,)), dma((2 * NZ,)),
            dma((2 * CHUNKS + 4,)), dma((2 * CHUNKS + 4,)), dma((RELAYED,)), dma((RELAYED,)), dma((2,)), dma((2,)), dma((8,)),
        ],
        compiler_params=pltpu.CompilerParams(
            collective_id=0, has_side_effects=True, vmem_limit_bytes=60 * 2**20
        ),
    )(
        support_tiles,
        potential.reshape(REG_ROWS, COLS),
        tile_region.reshape(1, COUNT),
        tile_block.reshape(1, COUNT),
        pair_atoms,
    )


def solution(mesh):
    placed = P(("grid", "atoms"))
    return jax.shard_map(
        shards,
        mesh=mesh,
        in_specs=(placed, P("grid"), placed, placed, placed),
        out_specs=(placed, placed, placed),
        check_vma=False,
    )
```

```python
import heapq

import jax
import jax.numpy as jnp
import numpy as np
from jax import lax
from jax.experimental import pallas as pl
from jax.experimental.pallas import tpu as pltpu
from jax.sharding import PartitionSpec as P

MESH = pl.DeviceIdType.MESH
F32, BF16, I32 = jnp.float32, jnp.bfloat16, jnp.int32
NZ, NX, NY = 8, 4, 4
DEVICES = NZ * NX * 2 * NY
COUNT, ROWS, COLS = 64, 160, 128
ATOMS, PAIRS, SPA = 16, 32, 4
REG_ROWS = 512
UP, DOWN = 96, 80
PITCH = 72
CUT = 80
SPLIT = 160
CHUNKS, RELAYED = 8, 4
CHUNK = COUNT // CHUNKS
SEND_AT = {4: 0, 5: 0, 6: 4, 7: 8, 0: 18, 1: 28, 2: 38, 3: 48}
RELAY_AT = {4: 20, 5: 28, 6: 36, 7: 44}
SIZE = {"A": SPLIT, "B": REG_ROWS - SPLIT}
BASE = {"A": 0, "B": SPLIT}


def plan():
    axes = {"A": "xz", "B": "zx"}
    length = {"x": NX, "z": NZ}
    free, ready, arrivals, met = {}, [], [], {}
    count = 0

    def push(t, cause, message):
        nonlocal count
        heapq.heappush(ready, (t, count, cause, message))
        count += 1

    def starts(t, cause, part, axis, dz, dx):
        for sign in (1, -1):
            push(t, cause, (part, axis, sign, dz, dx, "full"))

    for part in "AB":
        for axis in axes[part]:
            starts(0.0, None, part, axis, 0, 0)
    while ready:
        best = min(
            range(len(ready)),
            key=lambda i: (max(ready[i][0], free.get(ready[i][3][1:3], 0.0)), ready[i][1]),
        )
        t, _, cause, message = ready.pop(best)
        heapq.heapify(ready)
        part, axis, sign, dz, dx, extent = message
        rows = SIZE[part] if extent == "full" else SIZE[part] // 2
        end = max(t, free.get((axis, sign), 0.0)) + rows
        free[axis, sign] = end
        dz, dx = (dz - sign, dx) if axis == "z" else (dz, dx - sign)
        me, t = len(arrivals), end + 300
        arrivals.append((t, me, (part, axis, sign, dz, dx, extent), cause))
        steps, half = abs(dz if axis == "z" else dx), length[axis] // 2
        if extent == "full":
            push(t, me, (part, axis, sign, dz, dx, "full" if steps < half - 1 else "half"))
        if axis == axes[part][0]:
            key = (part, dz % NZ, dx % NX)
            if extent == "full" or key in met:
                starts(t, me, part, axes[part][1], dz, dx)
            met[key] = me
    return sorted(arrivals)


ORDER = plan()
PLACE = {arrival[1]: i for i, arrival in enumerate(ORDER)}
FOLLOW = {}
for i, arrival in enumerate(ORDER):
    FOLLOW.setdefault(None if arrival[3] is None else PLACE[arrival[3]], []).append(i)
for followers in FOLLOW.values():
    followers.sort(key=lambda i: ORDER[i][1])
WHOLE = {}
for i, arrival in enumerate(ORDER):
    WHOLE[arrival[2][0], arrival[2][3] % NZ] = i
COMPLETE = {}
for key, i in WHOLE.items():
    COMPLETE.setdefault(i, []).append(key)


def banded(rows, cols, shift=0):
    i = lax.broadcasted_iota(I32, (rows, cols), 0) + shift
    j = lax.broadcasted_iota(I32, (rows, cols), 1)
    return spread_values(jnp.abs(i - j))


def spread_values(spread):
    coeffs = np.array([-49.0 / 18.0, 1.5, -0.15, 1.0 / 90.0], np.float32)
    coeffs = -0.5 * coeffs.astype(BF16).astype(np.float32)
    out = jnp.zeros(spread.shape, F32)
    for k in range(4):
        out = jnp.where(spread == k, float(coeffs[k]), out)
    return out.astype(BF16)


def two_bands():
    i = lax.broadcasted_iota(I32, (2 * COLS, 2 * COLS), 0)
    j = lax.broadcasted_iota(I32, (2 * COLS, 2 * COLS), 1)
    return spread_values(jnp.where(i // COLS == j // COLS, jnp.abs(i - j), 9))


def cut(pot, region, block, first, rows):
    tile, shift = lax.shift_right_logical(block, 3) + first // 16, 2 * (block & 7)
    chip, core = lax.shift_right_logical(region, 1), region & 1
    parts = []
    for k in range(rows // 16 + 1):
        raw = pot[chip, core, lax.min(tile + k, REG_ROWS // 16 - 1)].astype(F32)
        parts += [raw[0:8], raw[8:16]]
    odd = shift >= 8
    parts = [jnp.where(odd, parts[k + 1], parts[k]) for k in range(rows // 8 + 1)]
    within = shift & 7
    parts = [pltpu.roll(part, (8 - within) & 7, axis=0) for part in parts]
    stays = lax.broadcasted_iota(I32, (8, COLS), 0) < 8 - within
    return jnp.concatenate([jnp.where(stays, parts[k], parts[k + 1]) for k in range(rows // 8)], axis=0)


def pair_of(x_ref, i):
    return [x_ref[2 * i], x_ref[2 * i + 1]]


def filtered(xs, skip, rows, krow, kcol):
    x = jnp.concatenate(xs, axis=1)
    rows_part = jnp.dot(krow[...], x, preferred_element_type=F32)
    return rows_part + jnp.dot(x[skip : skip + rows], kcol[...], preferred_element_type=F32)


def prepare(x_ref, rows, krow, kcol, kinetic, x_to, first, count):
    def body(i, _):
        xs = pair_of(x_ref, i)
        both = filtered(xs, 0, rows, krow, kcol)
        for h in range(2):
            kinetic[2 * i + h] = both[:, COLS * h : COLS * (h + 1)]
            x_to[pl.ds(2 * i + h, rows, stride=PITCH), :] = xs[h].astype(F32)
        return 0

    lax.fori_loop(first, first + count, body, 0, unroll=2)


def finish(x_ref, rows, pot, meta, line, kinetic, out, a_to):
    def body(f, _):
        local = cut(pot, meta[0, line, 0, f], meta[1, line, 0, f], 0, rows) * x_ref[f].astype(F32)
        a = (kinetic[f] + local).astype(BF16)
        out[f] = a
        a_to[pl.ds(f, rows, stride=PITCH), :] = a.astype(F32)
        return 0

    lax.fori_loop(0, COUNT, body, 0, unroll=2)


def apply_block(x_ref, first_in, rows_in, first_out, rows_out, krow, kcol, pot, meta, line, x_to, a_to):
    skip = first_out - first_in

    def body(i, _):
        xs = pair_of(x_ref, i)
        kinetic = filtered(xs, skip, rows_out, krow, kcol)
        for h in range(2):
            f = 2 * i + h
            window = cut(pot, meta[0, line, 0, f], meta[1, line, 0, f], first_out, rows_out)
            values = xs[h].astype(F32)
            a = kinetic[:, COLS * h : COLS * (h + 1)] + window * values[skip : skip + rows_out]
            a_to[pl.ds(f, rows_out, stride=PITCH), :] = a.astype(BF16).astype(F32)
            x_to[pl.ds(f, rows_in, stride=PITCH), :] = values
        return 0

    lax.fori_loop(0, COUNT // 2, body, 0, unroll=8)


def gram(first, last, lhs, rhs):
    def rows(refs, r):
        return jnp.concatenate(
            [
                jnp.concatenate(
                    [ref[pl.ds(pl.multiple_of((r + k - start) * PITCH, 8), COUNT), :].astype(BF16) for k in range(16)],
                    axis=1,
                )
                for ref, start in refs
            ],
            axis=0,
        )

    def body(i, total):
        r = first + 16 * i
        return total + lax.dot_general(
            rows(lhs, r), rows(rhs, r), (((1,), (1,)), ((), ())), preferred_element_type=F32
        )

    total = jnp.zeros((COUNT * len(lhs), COUNT * len(rhs)), F32)
    return lax.fori_loop(0, (last - first) // 16, body, total, unroll=4)


def lane_pick(x, lanes):
    return jnp.take_along_axis(x, lanes, axis=1, mode="promise_in_bounds")


def kernel(
    tiles_hbm, own_pot, region, block, pairs,
    applied_hbm, table, table_after, wanted,
    pot, tiles, prev, after, applied, krow, kcol, kinetic,
    t_rows, a_rows, tp_rows, ap_rows, tn_rows, an_rows,
    meta_v, meta, to_prev, to_next, from_prev, from_next,
    relay,
    send, recv, sib_send, sib_recv, halo_send, halo_recv, relay_send, relay_recv, small_send, small_recv, local_sem,
):
    g, y = lax.axis_index("grid"), lax.axis_index("atoms")
    z, x, c = g // 8, (g // 2) % 4, g % 2

    def chip(dz, dx):
        return ((z + dz + NZ) % NZ) * NX + (x + dx + NX) % NX

    def at(position):
        position = (position + DEVICES) % DEVICES
        return (position // NY, position % NY)

    me = g * NY + y
    near = {("z", s): (chip(s, 0) * 2 + c, y) for s in (1, -1)}
    near.update({("x", s): (chip(0, s) * 2 + c, y) for s in (1, -1)})
    sibling = (g + 1 - 2 * c, y)
    later, earlier = at(me + 1), at(me - 1)
    everyone = [*near.values(), sibling, later, earlier]
    barrier = pltpu.get_barrier_semaphore()
    for device in everyone:
        pl.semaphore_signal(barrier, inc=1, device_id=device, device_id_type=MESH)
    at_low, at_high = y == 0, y == NY - 1
    at_end = jnp.logical_or(at_low, at_high)
    side = 2 * (y // (NY - 1)) - 1
    opposite = (g, NY - 1 - y)
    onward, ward = ((g - side + 64) % 64, y), ((g + side + 64) % 64, y)

    @pl.when(at_end)
    def _():
        for device in (opposite, ward):
            pl.semaphore_signal(barrier, inc=1, device_id=device, device_id_type=MESH)

    def remote(src, dst, s, r, device):
        return pltpu.make_async_remote_copy(src, dst, s, r, device_id=device, device_id_type=MESH)

    tiles_in = pltpu.make_async_copy(tiles_hbm, tiles, local_sem.at[0])
    tiles_in.start()
    pot[chip(0, 0), c] = own_pot[...].astype(BF16).reshape(REG_ROWS // 16, 16, COLS)
    krow[...] = banded(ROWS, ROWS)
    kcol[...] = two_bands()
    @pl.when(at_end)
    def _():
        pl.semaphore_wait(barrier, len(everyone) + 2)

    @pl.when(jnp.logical_not(at_end))
    def _():
        pl.semaphore_wait(barrier, len(everyone))

    halos = [
        remote(region, meta_v.at[0], halo_send.at[2 * CHUNKS], halo_recv.at[2 * CHUNKS], later),
        remote(block, meta_v.at[1], halo_send.at[2 * CHUNKS + 1], halo_recv.at[2 * CHUNKS + 1], later),
        remote(region, meta_v.at[2], halo_send.at[2 * CHUNKS + 2], halo_recv.at[2 * CHUNKS + 2], earlier),
        remote(block, meta_v.at[3], halo_send.at[2 * CHUNKS + 3], halo_recv.at[2 * CHUNKS + 3], earlier),
    ]

    def chunk(k, up):
        some = pl.ds(k * CHUNK, CHUNK)
        if up:
            return remote(
                tiles_hbm.at[some, pl.ds(0, UP)], prev.at[some], halo_send.at[2 * k], halo_recv.at[2 * k], later
            )
        return remote(
            tiles_hbm.at[some, pl.ds(CUT, DOWN)], after.at[some], halo_send.at[2 * k + 1], halo_recv.at[2 * k + 1],
            earlier,
        )

    def slot(k, up):
        return relay.at[k - CHUNKS + RELAYED, :, pl.ds(0, UP if up else DOWN)]

    def detour(k, up):
        some = pl.ds(k * CHUNK, CHUNK)
        src = tiles_hbm.at[some, pl.ds(0, UP) if up else pl.ds(CUT, DOWN)]
        j = k - CHUNKS + RELAYED
        return remote(src, slot(k, up), halo_send.at[2 * k + 1 - up], relay_recv.at[j], opposite)

    def send_on(k, up):
        some = pl.ds(k * CHUNK, CHUNK)
        j = k - CHUNKS + RELAYED
        dst = prev.at[some] if up else after.at[some]
        return remote(slot(k, up), dst, relay_send.at[j], halo_recv.at[2 * k + 1 - up], onward)

    def send_chunk(k):
        if k < CHUNKS - RELAYED:
            chunk(k, 1).start()
            chunk(k, 0).start()
            return
        for up, edge in ((1, at_high), (0, at_low)):

            @pl.when(edge)
            def _():
                detour(k, up).start()

            @pl.when(jnp.logical_not(edge))
            def _():
                chunk(k, up).start()

    def relay_chunk(k):
        for up, edge in ((1, at_low), (0, at_high)):

            @pl.when(edge)
            def _():
                landed(slot(k, up), relay_recv.at[k - CHUNKS + RELAYED])
                send_on(k, up).start()

    def relay_sent(k):
        for up, edge in ((1, at_low), (0, at_high)):

            @pl.when(edge)
            def _():
                send_on(k, up).wait_send()

    def slab(part, dz, dx, sign, extent):
        low, rows = BASE[part], SIZE[part]
        if extent == "half":
            rows //= 2
            low += 0 if sign > 0 else rows
        return pot.at[chip(dz, dx), c, pl.ds(low // 16, rows // 16)]

    def forward(i):
        part, axis, sign, dz, dx, extent = ORDER[i][2]
        dz, dx = (dz + sign, dx) if axis == "z" else (dz, dx + sign)
        src = slab(part, dz, dx, sign, extent)
        return remote(src, src, send.at[i], recv.at[i], near[axis, sign])

    def plane(key, core):
        part, dz = key
        return pot.at[pl.ds(((z + dz) % NZ) * NX, NX), core, pl.ds(BASE[part] // 16, SIZE[part] // 16)]

    def hand_over(key):
        j = "AB".index(key[0]) * NZ + key[1]
        return remote(plane(key, c), plane(key, c), sib_send.at[j], sib_recv.at[j], sibling)

    def landed(ref, sem):
        pltpu.make_async_copy(ref, ref, sem).wait()

    for i in FOLLOW[None]:
        forward(i).start()
    for copy in halos:
        copy.start()
    for k, when in SEND_AT.items():
        if when == 0:
            send_chunk(k)
    own_meta = [
        pltpu.make_async_copy(region, meta.at[0, 0], local_sem.at[1]),
        pltpu.make_async_copy(block, meta.at[1, 0], local_sem.at[2]),
    ]
    for copy in own_meta:
        copy.start()
    handed = []
    done = 0
    for i in range(len(ORDER)):
        part, axis, sign, dz, dx, extent = ORDER[i][2]
        landed(slab(part, dz, dx, sign, extent), recv.at[i])
        for j in FOLLOW.get(i, []):
            forward(j).start()
        for key in COMPLETE.get(i, []):
            hand_over(key).start()
            handed.append(key)
        for k, when in SEND_AT.items():
            if when == i + 1:
                send_chunk(k)
        for k, when in RELAY_AT.items():
            if when == i + 1:
                relay_chunk(k)
        if i == 7:
            tiles_in.wait()
        if i >= 8 and i % 2 == 0 and done < COUNT // 2:
            prepare(tiles, ROWS, krow, kcol, kinetic, t_rows, done, 2)
            done += 2
    for key in handed:
        landed(plane(key, 1 - c), sib_recv.at["AB".index(key[0]) * NZ + key[1]])
    for copy in own_meta:
        copy.wait()
    finish(tiles, ROWS, pot, meta, 0, kinetic, applied, a_rows)
    out = pltpu.make_async_copy(applied, applied_hbm, local_sem.at[3])
    out.start()
    for copy in halos:
        copy.wait()
    for k in range(CHUNKS):
        chunk(k, 1).wait()
        chunk(k, 0).wait()
    metas = [pltpu.make_async_copy(meta_v.at[k], meta.at[k % 2, 1 + k // 2], local_sem.at[4 + k]) for k in range(4)]
    for copy in metas:
        copy.start()
    for copy in metas:
        copy.wait()
    apply_block(
        prev, 0, UP, 0, CUT, krow.at[0:CUT, 0:UP], kcol, pot, meta, 1, tp_rows, ap_rows
    )
    apply_block(
        after, CUT, DOWN, UP, ROWS - UP, krow.at[UP:ROWS, CUT:ROWS], kcol, pot, meta, 2,
        tn_rows, an_rows,
    )
    own = [(t_rows, 0), (a_rows, 0)]
    low = gram(0, CUT, own, [(t_rows, 0), (tp_rows, 0), (ap_rows, 0)])
    mid = gram(CUT, UP, own, [(t_rows, 0), (tp_rows, 0), (tn_rows, CUT)])
    high = gram(UP, ROWS, own, [(t_rows, 0), (tn_rows, CUT), (an_rows, UP)])
    to_prev[...] = low[0:COUNT, COUNT:]
    to_next[...] = high[0:COUNT, COUNT:]
    to_prev[:, 0:COUNT] = low[0:COUNT, COUNT : 2 * COUNT] + mid[0:COUNT, COUNT : 2 * COUNT]
    results = [
        remote(to_prev, from_next, small_send.at[0], small_recv.at[0], earlier),
        remote(to_next, from_prev, small_send.at[1], small_recv.at[1], later),
    ]
    for copy in results:
        copy.start()
    scale = float(ROWS * COLS) ** -0.5
    one, two, three = slice(0, COUNT), slice(COUNT, 2 * COUNT), slice(2 * COUNT, 3 * COUNT)
    table[:, two] = (low[:, one] + mid[:, one] + high[:, one]) * scale
    lanes = lax.broadcasted_iota(I32, (ATOMS, COLS), 1)
    wide = jnp.concatenate([pairs[...]] * (COLS // PAIRS), axis=1)
    first = (me - 1) * ATOMS
    for k in range(SPA):
        partner = lane_pick(wide, lanes // 16 + 8 * k)
        column = ((partner - first + 2 * DEVICES * ATOMS) % (DEVICES * ATOMS)) * SPA + lanes % SPA
        wanted[:, k * COLS : (k + 1) * COLS] = column
    for copy in results:
        copy.wait()
    table[:, one] = (low[:, two] + mid[:, two] + from_prev[...].T) * scale
    table_after[...] = jnp.zeros_like(table_after)
    table_after[0:COUNT, one] = (high[0:COUNT, two] + from_next[...].T[0:COUNT]) * scale
    table_after[COUNT : 2 * COUNT, one] = (
        high[COUNT : 2 * COUNT, two] + mid[COUNT : 2 * COUNT, three] + from_next[...].T[COUNT : 2 * COUNT]
    ) * scale
    for i in range(len(ORDER)):
        forward(i).wait_send()
    for key in handed:
        hand_over(key).wait_send()
    for k in RELAY_AT:
        relay_sent(k)
    out.wait()


PIECES = 8


def pick(applied_in, table, table_after, wanted, applied, margin, hamiltonian, sem):
    some = COUNT // PIECES
    copies = [
        pltpu.make_async_copy(applied_in.at[pl.ds(k * some, some)], applied.at[pl.ds(k * some, some)], sem.at[k])
        for k in range(PIECES)
    ]
    for copy in copies:
        copy.start()
    lanes = lax.broadcasted_iota(I32, (ATOMS, COLS), 1)
    for k, target in ((0, margin), (1, hamiltonian)):
        for q in range(SPA):
            total = jnp.zeros((ATOMS, COLS), F32)
            for s in range(SPA):
                rows = pl.ds(k * COUNT + s, ATOMS, stride=SPA)
                left, right = table[rows, :], table_after[rows, :]
                column = wanted[:, q * COLS : (q + 1) * COLS]
                inside = column % COLS
                value = jnp.where(column < COLS, lane_pick(left, inside), lane_pick(right, inside))
                total = jnp.where((lanes // SPA) % SPA == s, value, total)
            target[:, q * COLS : (q + 1) * COLS] = total
    for copy in copies:
        copy.wait()


def shards(support_tiles, potential, tile_region, tile_block, pair_atoms):
    vmem, hbm = pl.BlockSpec(memory_space=pltpu.VMEM), pl.BlockSpec(memory_space=pl.ANY)
    dma = pltpu.SemaphoreType.DMA
    messages = len(ORDER)
    served = pl.pallas_call(
        kernel,
        out_shape=(
            jax.ShapeDtypeStruct((COUNT, ROWS, COLS), BF16),
            jax.ShapeDtypeStruct((2 * COUNT, COLS), F32),
            jax.ShapeDtypeStruct((2 * COUNT, COLS), F32),
            jax.ShapeDtypeStruct((ATOMS, PAIRS * SPA * SPA), I32),
        ),
        in_specs=[hbm, vmem, vmem, vmem, vmem],
        out_specs=(hbm, vmem, vmem, vmem),
        scratch_shapes=[
            pltpu.VMEM((NZ * NX, 2, REG_ROWS // 16, 16, COLS), BF16),
            pltpu.VMEM((COUNT, ROWS, COLS), BF16),
            pltpu.VMEM((COUNT, UP, COLS), BF16),
            pltpu.VMEM((COUNT, DOWN, COLS), BF16),
            pltpu.VMEM((COUNT, ROWS, COLS), BF16),
            pltpu.VMEM((ROWS, ROWS), BF16),
            pltpu.VMEM((2 * COLS, 2 * COLS), BF16),
            pltpu.VMEM((COUNT, ROWS, COLS), F32),
            *[pltpu.VMEM((rows * PITCH, COLS), F32) for rows in (ROWS, ROWS, UP, CUT, DOWN, ROWS - UP)],
            pltpu.VMEM((4, 1, COUNT), I32),
            pltpu.SMEM((2, 3, 1, COUNT), I32),
            *[pltpu.VMEM((COUNT, 2 * COUNT), F32) for _ in range(4)],
            pltpu.VMEM((RELAYED, CHUNK, UP, COLS), BF16),
            dma((messages,)), dma((messages,)), dma((2 * NZ,)), dma((2 * NZ,)),
            dma((2 * CHUNKS + 4,)), dma((2 * CHUNKS + 4,)), dma((RELAYED,)), dma((RELAYED,)), dma((2,)), dma((2,)), dma((8,)),
        ],
        compiler_params=pltpu.CompilerParams(
            collective_id=0, has_side_effects=True, vmem_limit_bytes=60 * 2**20
        ),
    )(
        support_tiles,
        potential.reshape(REG_ROWS, COLS),
        tile_region.reshape(1, COUNT),
        tile_block.reshape(1, COUNT),
        pair_atoms,
    )
    blocks = jax.ShapeDtypeStruct((ATOMS, PAIRS * SPA * SPA), F32)
    return pl.pallas_call(
        pick,
        out_shape=(jax.ShapeDtypeStruct((COUNT, ROWS, COLS), BF16), blocks, blocks),
        in_specs=[hbm, vmem, vmem, vmem],
        out_specs=(hbm, vmem, vmem),
        scratch_shapes=[dma((PIECES,))],
        compiler_params=pltpu.CompilerParams(vmem_limit_bytes=60 * 2**20),
    )(*served)


def solution(mesh):
    placed = P(("grid", "atoms"))
    return jax.shard_map(
        shards,
        mesh=mesh,
        in_specs=(placed, P("grid"), placed, placed, placed),
        out_specs=(placed, placed, placed),
        check_vma=False,
    )
```

```python
import heapq

import jax
import jax.numpy as jnp
import numpy as np
from jax import lax
from jax.experimental import pallas as pl
from jax.experimental.pallas import tpu as pltpu
from jax.sharding import PartitionSpec as P

MESH = pl.DeviceIdType.MESH
F32, BF16, I32 = jnp.float32, jnp.bfloat16, jnp.int32
NZ, NX, NY = 8, 4, 4
DEVICES = NZ * NX * 2 * NY
COUNT, ROWS, COLS = 64, 160, 128
ATOMS, PAIRS, SPA = 16, 32, 4
REG_ROWS = 512
UP, DOWN = 96, 80
PITCH = 72
CUT = 80
SPLIT = 160
CHUNKS, RELAYED = 8, 4
CHUNK = COUNT // CHUNKS
SEND_AT = {4: 0, 5: 0, 6: 4, 7: 8, 0: 18, 1: 28, 2: 38, 3: 48}
RELAY_AT = {4: 20, 5: 28, 6: 36, 7: 44}
SIZE = {"A": SPLIT, "B": REG_ROWS - SPLIT}
BASE = {"A": 0, "B": SPLIT}


def plan():
    axes = {"A": "xz", "B": "zx"}
    length = {"x": NX, "z": NZ}
    free, ready, arrivals, met = {}, [], [], {}
    count = 0

    def push(t, cause, message):
        nonlocal count
        heapq.heappush(ready, (t, count, cause, message))
        count += 1

    def starts(t, cause, part, axis, dz, dx):
        for sign in (1, -1):
            push(t, cause, (part, axis, sign, dz, dx, "full"))

    for part in "AB":
        for axis in axes[part]:
            starts(0.0, None, part, axis, 0, 0)
    while ready:
        best = min(
            range(len(ready)),
            key=lambda i: (max(ready[i][0], free.get(ready[i][3][1:3], 0.0)), ready[i][1]),
        )
        t, _, cause, message = ready.pop(best)
        heapq.heapify(ready)
        part, axis, sign, dz, dx, extent = message
        rows = SIZE[part] if extent == "full" else SIZE[part] // 2
        end = max(t, free.get((axis, sign), 0.0)) + rows
        free[axis, sign] = end
        dz, dx = (dz - sign, dx) if axis == "z" else (dz, dx - sign)
        me, t = len(arrivals), end + 300
        arrivals.append((t, me, (part, axis, sign, dz, dx, extent), cause))
        steps, half = abs(dz if axis == "z" else dx), length[axis] // 2
        if extent == "full":
            push(t, me, (part, axis, sign, dz, dx, "full" if steps < half - 1 else "half"))
        if axis == axes[part][0]:
            key = (part, dz % NZ, dx % NX)
            if extent == "full" or key in met:
                starts(t, me, part, axes[part][1], dz, dx)
            met[key] = me
    return sorted(arrivals)


ORDER = plan()
PLACE = {arrival[1]: i for i, arrival in enumerate(ORDER)}
FOLLOW = {}
for i, arrival in enumerate(ORDER):
    FOLLOW.setdefault(None if arrival[3] is None else PLACE[arrival[3]], []).append(i)
for followers in FOLLOW.values():
    followers.sort(key=lambda i: ORDER[i][1])
WHOLE = {}
for i, arrival in enumerate(ORDER):
    WHOLE[arrival[2][0], arrival[2][3] % NZ] = i
COMPLETE = {}
for key, i in WHOLE.items():
    COMPLETE.setdefault(i, []).append(key)


def banded(rows, cols, shift=0):
    i = lax.broadcasted_iota(I32, (rows, cols), 0) + shift
    j = lax.broadcasted_iota(I32, (rows, cols), 1)
    return spread_values(jnp.abs(i - j))


def spread_values(spread):
    coeffs = np.array([-49.0 / 18.0, 1.5, -0.15, 1.0 / 90.0], np.float32)
    coeffs = -0.5 * coeffs.astype(BF16).astype(np.float32)
    out = jnp.zeros(spread.shape, F32)
    for k in range(4):
        out = jnp.where(spread == k, float(coeffs[k]), out)
    return out.astype(BF16)


def two_bands():
    i = lax.broadcasted_iota(I32, (2 * COLS, 2 * COLS), 0)
    j = lax.broadcasted_iota(I32, (2 * COLS, 2 * COLS), 1)
    return spread_values(jnp.where(i // COLS == j // COLS, jnp.abs(i - j), 9))


def cut(pot, region, block, first, rows):
    tile, shift = lax.shift_right_logical(block, 3) + first // 16, 2 * (block & 7)
    chip, core = lax.shift_right_logical(region, 1), region & 1
    parts = []
    for k in range(rows // 16 + 1):
        raw = pot[chip, core, lax.min(tile + k, REG_ROWS // 16 - 1)].astype(F32)
        parts += [raw[0:8], raw[8:16]]
    odd = shift >= 8
    parts = [jnp.where(odd, parts[k + 1], parts[k]) for k in range(rows // 8 + 1)]
    within = shift & 7
    parts = [pltpu.roll(part, (8 - within) & 7, axis=0) for part in parts]
    stays = lax.broadcasted_iota(I32, (8, COLS), 0) < 8 - within
    return jnp.concatenate([jnp.where(stays, parts[k], parts[k + 1]) for k in range(rows // 8)], axis=0)


def pair_of(x_ref, i):
    return [x_ref[2 * i], x_ref[2 * i + 1]]


def filtered(xs, skip, rows, krow, kcol):
    x = jnp.concatenate(xs, axis=1)
    rows_part = jnp.dot(krow[...], x, preferred_element_type=F32)
    return rows_part + jnp.dot(x[skip : skip + rows], kcol[...], preferred_element_type=F32)


def prepare(x_ref, rows, krow, kcol, kinetic, x_to, first, count):
    def body(i, _):
        xs = pair_of(x_ref, i)
        both = filtered(xs, 0, rows, krow, kcol)
        for h in range(2):
            kinetic[2 * i + h] = both[:, COLS * h : COLS * (h + 1)]
            x_to[pl.ds(2 * i + h, rows, stride=PITCH), :] = xs[h].astype(F32)
        return 0

    lax.fori_loop(first, first + count, body, 0, unroll=2)


def finish(x_ref, rows, pot, meta, line, kinetic, out, a_to):
    def body(f, _):
        local = cut(pot, meta[0, line, 0, f], meta[1, line, 0, f], 0, rows) * x_ref[f].astype(F32)
        a = (kinetic[f] + local).astype(BF16)
        out[f] = a
        a_to[pl.ds(f, rows, stride=PITCH), :] = a.astype(F32)
        return 0

    lax.fori_loop(0, COUNT, body, 0, unroll=2)


def apply_block(x_ref, first_in, rows_in, first_out, rows_out, krow, kcol, pot, meta, line, x_to, a_to):
    skip = first_out - first_in

    def body(i, _):
        xs = pair_of(x_ref, i)
        kinetic = filtered(xs, skip, rows_out, krow, kcol)
        for h in range(2):
            f = 2 * i + h
            window = cut(pot, meta[0, line, 0, f], meta[1, line, 0, f], first_out, rows_out)
            values = xs[h].astype(F32)
            a = kinetic[:, COLS * h : COLS * (h + 1)] + window * values[skip : skip + rows_out]
            a_to[pl.ds(f, rows_out, stride=PITCH), :] = a.astype(BF16).astype(F32)
            x_to[pl.ds(f, rows_in, stride=PITCH), :] = values
        return 0

    lax.fori_loop(0, COUNT // 2, body, 0, unroll=8)


def gram(first, last, lhs, rhs):
    def rows(refs, r):
        return jnp.concatenate(
            [
                jnp.concatenate(
                    [ref[pl.ds(pl.multiple_of((r + k - start) * PITCH, 8), COUNT), :].astype(BF16) for k in range(16)],
                    axis=1,
                )
                for ref, start in refs
            ],
            axis=0,
        )

    def body(i, total):
        r = first + 16 * i
        return total + lax.dot_general(
            rows(lhs, r), rows(rhs, r), (((1,), (1,)), ((), ())), preferred_element_type=F32
        )

    total = jnp.zeros((COUNT * len(lhs), COUNT * len(rhs)), F32)
    return lax.fori_loop(0, (last - first) // 16, body, total, unroll=4)


def lane_pick(x, lanes):
    return jnp.take_along_axis(x, lanes, axis=1, mode="promise_in_bounds")


def kernel(
    tiles_hbm, own_pot, region, block, pairs,
    applied_hbm, table, table_after, wanted,
    pot, tiles, prev, after, applied, krow, kcol, kinetic,
    t_rows, a_rows, tp_rows, ap_rows, tn_rows, an_rows,
    meta_v, meta, to_prev, to_next, from_prev, from_next,
    relay,
    send, recv, sib_send, sib_recv, halo_send, halo_recv, relay_send, relay_recv, small_send, small_recv, local_sem,
):
    g, y = lax.axis_index("grid"), lax.axis_index("atoms")
    z, x, c = g // 8, (g // 2) % 4, g % 2

    def chip(dz, dx):
        return ((z + dz + NZ) % NZ) * NX + (x + dx + NX) % NX

    def at(position):
        position = (position + DEVICES) % DEVICES
        return (position // NY, position % NY)

    me = g * NY + y
    near = {("z", s): (chip(s, 0) * 2 + c, y) for s in (1, -1)}
    near.update({("x", s): (chip(0, s) * 2 + c, y) for s in (1, -1)})
    sibling = (g + 1 - 2 * c, y)
    later, earlier = at(me + 1), at(me - 1)
    everyone = [*near.values(), sibling, later, earlier]
    barrier = pltpu.get_barrier_semaphore()
    for device in everyone:
        pl.semaphore_signal(barrier, inc=1, device_id=device, device_id_type=MESH)
    at_low, at_high = y == 0, y == NY - 1
    at_end = jnp.logical_or(at_low, at_high)
    side = 2 * (y // (NY - 1)) - 1
    opposite = (g, NY - 1 - y)
    onward, ward = ((g - side + 64) % 64, y), ((g + side + 64) % 64, y)

    @pl.when(at_end)
    def _():
        for device in (opposite, ward):
            pl.semaphore_signal(barrier, inc=1, device_id=device, device_id_type=MESH)

    def remote(src, dst, s, r, device):
        return pltpu.make_async_remote_copy(src, dst, s, r, device_id=device, device_id_type=MESH)

    tiles_in = pltpu.make_async_copy(tiles_hbm, tiles, local_sem.at[0])
    tiles_in.start()
    pot[chip(0, 0), c] = own_pot[...].astype(BF16).reshape(REG_ROWS // 16, 16, COLS)
    krow[...] = banded(ROWS, ROWS)
    kcol[...] = two_bands()
    @pl.when(at_end)
    def _():
        pl.semaphore_wait(barrier, len(everyone) + 2)

    @pl.when(jnp.logical_not(at_end))
    def _():
        pl.semaphore_wait(barrier, len(everyone))

    halos = [
        remote(region, meta_v.at[0], halo_send.at[2 * CHUNKS], halo_recv.at[2 * CHUNKS], later),
        remote(block, meta_v.at[1], halo_send.at[2 * CHUNKS + 1], halo_recv.at[2 * CHUNKS + 1], later),
        remote(region, meta_v.at[2], halo_send.at[2 * CHUNKS + 2], halo_recv.at[2 * CHUNKS + 2], earlier),
        remote(block, meta_v.at[3], halo_send.at[2 * CHUNKS + 3], halo_recv.at[2 * CHUNKS + 3], earlier),
    ]

    def chunk(k, up):
        some = pl.ds(k * CHUNK, CHUNK)
        if up:
            return remote(
                tiles_hbm.at[some, pl.ds(0, UP)], prev.at[some], halo_send.at[2 * k], halo_recv.at[2 * k], later
            )
        return remote(
            tiles_hbm.at[some, pl.ds(CUT, DOWN)], after.at[some], halo_send.at[2 * k + 1], halo_recv.at[2 * k + 1],
            earlier,
        )

    def slot(k, up):
        return relay.at[k - CHUNKS + RELAYED, :, pl.ds(0, UP if up else DOWN)]

    def detour(k, up):
        some = pl.ds(k * CHUNK, CHUNK)
        src = tiles_hbm.at[some, pl.ds(0, UP) if up else pl.ds(CUT, DOWN)]
        j = k - CHUNKS + RELAYED
        return remote(src, slot(k, up), halo_send.at[2 * k + 1 - up], relay_recv.at[j], opposite)

    def send_on(k, up):
        some = pl.ds(k * CHUNK, CHUNK)
        j = k - CHUNKS + RELAYED
        dst = prev.at[some] if up else after.at[some]
        return remote(slot(k, up), dst, relay_send.at[j], halo_recv.at[2 * k + 1 - up], onward)

    def send_chunk(k):
        if k < CHUNKS - RELAYED:
            chunk(k, 1).start()
            chunk(k, 0).start()
            return
        for up, edge in ((1, at_high), (0, at_low)):

            @pl.when(edge)
            def _():
                detour(k, up).start()

            @pl.when(jnp.logical_not(edge))
            def _():
                chunk(k, up).start()

    def relay_chunk(k):
        for up, edge in ((1, at_low), (0, at_high)):

            @pl.when(edge)
            def _():
                landed(slot(k, up), relay_recv.at[k - CHUNKS + RELAYED])
                send_on(k, up).start()

    def relay_sent(k):
        for up, edge in ((1, at_low), (0, at_high)):

            @pl.when(edge)
            def _():
                send_on(k, up).wait_send()

    def slab(part, dz, dx, sign, extent):
        low, rows = BASE[part], SIZE[part]
        if extent == "half":
            rows //= 2
            low += 0 if sign > 0 else rows
        return pot.at[chip(dz, dx), c, pl.ds(low // 16, rows // 16)]

    def forward(i):
        part, axis, sign, dz, dx, extent = ORDER[i][2]
        dz, dx = (dz + sign, dx) if axis == "z" else (dz, dx + sign)
        src = slab(part, dz, dx, sign, extent)
        return remote(src, src, send.at[i], recv.at[i], near[axis, sign])

    def plane(key, core):
        part, dz = key
        return pot.at[pl.ds(((z + dz) % NZ) * NX, NX), core, pl.ds(BASE[part] // 16, SIZE[part] // 16)]

    def hand_over(key):
        j = "AB".index(key[0]) * NZ + key[1]
        return remote(plane(key, c), plane(key, c), sib_send.at[j], sib_recv.at[j], sibling)

    def landed(ref, sem):
        pltpu.make_async_copy(ref, ref, sem).wait()

    for i in FOLLOW[None]:
        forward(i).start()
    for copy in halos:
        copy.start()
    for k, when in SEND_AT.items():
        if when == 0:
            send_chunk(k)
    own_meta = [
        pltpu.make_async_copy(region, meta.at[0, 0], local_sem.at[1]),
        pltpu.make_async_copy(block, meta.at[1, 0], local_sem.at[2]),
    ]
    for copy in own_meta:
        copy.start()
    handed = []
    done = 0
    for i in range(len(ORDER)):
        part, axis, sign, dz, dx, extent = ORDER[i][2]
        landed(slab(part, dz, dx, sign, extent), recv.at[i])
        for j in FOLLOW.get(i, []):
            forward(j).start()
        for key in COMPLETE.get(i, []):
            hand_over(key).start()
            handed.append(key)
        for k, when in SEND_AT.items():
            if when == i + 1:
                send_chunk(k)
        for k, when in RELAY_AT.items():
            if when == i + 1:
                relay_chunk(k)
        if i == 7:
            tiles_in.wait()
        if i >= 8 and i % 2 == 0 and done < COUNT // 2:
            prepare(tiles, ROWS, krow, kcol, kinetic, t_rows, done, 2)
            done += 2
    for key in handed:
        landed(plane(key, 1 - c), sib_recv.at["AB".index(key[0]) * NZ + key[1]])
    for copy in own_meta:
        copy.wait()
    finish(tiles, ROWS, pot, meta, 0, kinetic, applied, a_rows)
    out = pltpu.make_async_copy(applied, applied_hbm, local_sem.at[3])
    out.start()
    for copy in halos:
        copy.wait()
    for k in range(CHUNKS):
        chunk(k, 1).wait()
        chunk(k, 0).wait()
    metas = [pltpu.make_async_copy(meta_v.at[k], meta.at[k % 2, 1 + k // 2], local_sem.at[4 + k]) for k in range(4)]
    for copy in metas:
        copy.start()
    for copy in metas:
        copy.wait()
    apply_block(
        prev, 0, UP, 0, CUT, krow.at[0:CUT, 0:UP], kcol, pot, meta, 1, tp_rows, ap_rows
    )
    apply_block(
        after, CUT, DOWN, UP, ROWS - UP, krow.at[UP:ROWS, CUT:ROWS], kcol, pot, meta, 2,
        tn_rows, an_rows,
    )
    own = [(t_rows, 0), (a_rows, 0)]
    low = gram(0, CUT, own, [(t_rows, 0), (tp_rows, 0), (ap_rows, 0)])
    mid = gram(CUT, UP, own, [(t_rows, 0), (tp_rows, 0), (tn_rows, CUT)])
    high = gram(UP, ROWS, own, [(t_rows, 0), (tn_rows, CUT), (an_rows, UP)])
    to_prev[...] = low[0:COUNT, COUNT:]
    to_next[...] = high[0:COUNT, COUNT:]
    to_prev[:, 0:COUNT] = low[0:COUNT, COUNT : 2 * COUNT] + mid[0:COUNT, COUNT : 2 * COUNT]
    results = [
        remote(to_prev, from_next, small_send.at[0], small_recv.at[0], earlier),
        remote(to_next, from_prev, small_send.at[1], small_recv.at[1], later),
    ]
    for copy in results:
        copy.start()
    scale = float(ROWS * COLS) ** -0.5
    one, two, three = slice(0, COUNT), slice(COUNT, 2 * COUNT), slice(2 * COUNT, 3 * COUNT)
    table[:, two] = (low[:, one] + mid[:, one] + high[:, one]) * scale
    lanes = lax.broadcasted_iota(I32, (ATOMS, COLS), 1)
    wide = jnp.concatenate([pairs[...]] * (COLS // PAIRS), axis=1)
    first = (me - 1) * ATOMS
    for k in range(SPA):
        partner = lane_pick(wide, lanes // 16 + 8 * k)
        column = ((partner - first + 2 * DEVICES * ATOMS) % (DEVICES * ATOMS)) * SPA + lanes % SPA
        wanted[:, k * COLS : (k + 1) * COLS] = column
    for copy in results:
        copy.wait()
    table[:, one] = (low[:, two] + mid[:, two] + from_prev[...].T) * scale
    table_after[...] = jnp.zeros_like(table_after)
    table_after[0:COUNT, one] = (high[0:COUNT, two] + from_next[...].T[0:COUNT]) * scale
    table_after[COUNT : 2 * COUNT, one] = (
        high[COUNT : 2 * COUNT, two] + mid[COUNT : 2 * COUNT, three] + from_next[...].T[COUNT : 2 * COUNT]
    ) * scale
    for i in range(len(ORDER)):
        forward(i).wait_send()
    for key in handed:
        hand_over(key).wait_send()
    for k in RELAY_AT:
        relay_sent(k)
    out.wait()


PIECES = 8


def pick(applied_in, table, table_after, wanted, applied, margin, hamiltonian, held, sem):
    some = COUNT // PIECES
    pieces = [pl.ds(k * some, some) for k in range(PIECES)]
    inward = [pltpu.make_async_copy(applied_in.at[at], held.at[at], sem.at[0, k]) for k, at in enumerate(pieces)]
    outward = [pltpu.make_async_copy(held.at[at], applied.at[at], sem.at[1, k]) for k, at in enumerate(pieces)]
    for copy in inward:
        copy.start()
    for k in range(PIECES):
        inward[k].wait()
        outward[k].start()
    lanes = lax.broadcasted_iota(I32, (ATOMS, COLS), 1)
    for k, target in ((0, margin), (1, hamiltonian)):
        for q in range(SPA):
            total = jnp.zeros((ATOMS, COLS), F32)
            for s in range(SPA):
                rows = pl.ds(k * COUNT + s, ATOMS, stride=SPA)
                left, right = table[rows, :], table_after[rows, :]
                column = wanted[:, q * COLS : (q + 1) * COLS]
                inside = column % COLS
                value = jnp.where(column < COLS, lane_pick(left, inside), lane_pick(right, inside))
                total = jnp.where((lanes // SPA) % SPA == s, value, total)
            target[:, q * COLS : (q + 1) * COLS] = total
    for copy in outward:
        copy.wait()


def shards(support_tiles, potential, tile_region, tile_block, pair_atoms):
    vmem, hbm = pl.BlockSpec(memory_space=pltpu.VMEM), pl.BlockSpec(memory_space=pl.ANY)
    dma = pltpu.SemaphoreType.DMA
    messages = len(ORDER)
    served = pl.pallas_call(
        kernel,
        out_shape=(
            jax.ShapeDtypeStruct((COUNT, ROWS, COLS), BF16),
            jax.ShapeDtypeStruct((2 * COUNT, COLS), F32),
            jax.ShapeDtypeStruct((2 * COUNT, COLS), F32),
            jax.ShapeDtypeStruct((ATOMS, PAIRS * SPA * SPA), I32),
        ),
        in_specs=[hbm, vmem, vmem, vmem, vmem],
        out_specs=(hbm, vmem, vmem, vmem),
        scratch_shapes=[
            pltpu.VMEM((NZ * NX, 2, REG_ROWS // 16, 16, COLS), BF16),
            pltpu.VMEM((COUNT, ROWS, COLS), BF16),
            pltpu.VMEM((COUNT, UP, COLS), BF16),
            pltpu.VMEM((COUNT, DOWN, COLS), BF16),
            pltpu.VMEM((COUNT, ROWS, COLS), BF16),
            pltpu.VMEM((ROWS, ROWS), BF16),
            pltpu.VMEM((2 * COLS, 2 * COLS), BF16),
            pltpu.VMEM((COUNT, ROWS, COLS), F32),
            *[pltpu.VMEM((rows * PITCH, COLS), F32) for rows in (ROWS, ROWS, UP, CUT, DOWN, ROWS - UP)],
            pltpu.VMEM((4, 1, COUNT), I32),
            pltpu.SMEM((2, 3, 1, COUNT), I32),
            *[pltpu.VMEM((COUNT, 2 * COUNT), F32) for _ in range(4)],
            pltpu.VMEM((RELAYED, CHUNK, UP, COLS), BF16),
            dma((messages,)), dma((messages,)), dma((2 * NZ,)), dma((2 * NZ,)),
            dma((2 * CHUNKS + 4,)), dma((2 * CHUNKS + 4,)), dma((RELAYED,)), dma((RELAYED,)), dma((2,)), dma((2,)), dma((8,)),
        ],
        compiler_params=pltpu.CompilerParams(
            collective_id=0, has_side_effects=True, vmem_limit_bytes=60 * 2**20
        ),
    )(
        support_tiles,
        potential.reshape(REG_ROWS, COLS),
        tile_region.reshape(1, COUNT),
        tile_block.reshape(1, COUNT),
        pair_atoms,
    )
    blocks = jax.ShapeDtypeStruct((ATOMS, PAIRS * SPA * SPA), F32)
    return pl.pallas_call(
        pick,
        out_shape=(jax.ShapeDtypeStruct((COUNT, ROWS, COLS), BF16), blocks, blocks),
        in_specs=[hbm, vmem, vmem, vmem],
        out_specs=(hbm, vmem, vmem),
        scratch_shapes=[pltpu.VMEM((COUNT, ROWS, COLS), BF16), dma((2, PIECES))],
        compiler_params=pltpu.CompilerParams(vmem_limit_bytes=60 * 2**20),
    )(*served)


def solution(mesh):
    placed = P(("grid", "atoms"))
    return jax.shard_map(
        shards,
        mesh=mesh,
        in_specs=(placed, P("grid"), placed, placed, placed),
        out_specs=(placed, placed, placed),
        check_vma=False,
    )
```

```python
import heapq

import jax
import jax.numpy as jnp
import numpy as np
from jax import lax
from jax.experimental import pallas as pl
from jax.experimental.pallas import tpu as pltpu
from jax.sharding import PartitionSpec as P

MESH = pl.DeviceIdType.MESH
F32, BF16, I32 = jnp.float32, jnp.bfloat16, jnp.int32
NZ, NX, NY = 8, 4, 4
DEVICES = NZ * NX * 2 * NY
COUNT, ROWS, COLS = 64, 160, 128
ATOMS, PAIRS, SPA = 16, 32, 4
REG_ROWS = 512
UP, DOWN = 96, 80
PITCH = 72
CUT = 80
SPLIT = 160
CHUNKS, RELAYED = 8, 4
CHUNK = COUNT // CHUNKS
SEND_AT = {4: 0, 5: 0, 6: 4, 7: 8, 0: 22, 1: 34, 2: 46, 3: 58}
RELAY_AT = {4: 20, 5: 30, 6: 40, 7: 50}
SIZE = {"A": SPLIT, "B": REG_ROWS - SPLIT}
BASE = {"A": 0, "B": SPLIT}


def plan():
    axes = {"A": "xz", "B": "zx"}
    length = {"x": NX, "z": NZ}
    free, ready, arrivals, met = {}, [], [], {}
    count = 0

    def push(t, cause, message):
        nonlocal count
        heapq.heappush(ready, (t, count, cause, message))
        count += 1

    def starts(t, cause, part, axis, dz, dx):
        for sign in (1, -1):
            push(t, cause, (part, axis, sign, dz, dx, "full"))

    for part in "AB":
        for axis in axes[part]:
            starts(0.0, None, part, axis, 0, 0)
    while ready:
        best = min(
            range(len(ready)),
            key=lambda i: (max(ready[i][0], free.get(ready[i][3][1:3], 0.0)), ready[i][1]),
        )
        t, _, cause, message = ready.pop(best)
        heapq.heapify(ready)
        part, axis, sign, dz, dx, extent = message
        rows = SIZE[part] if extent == "full" else SIZE[part] // 2
        end = max(t, free.get((axis, sign), 0.0)) + rows
        free[axis, sign] = end
        dz, dx = (dz - sign, dx) if axis == "z" else (dz, dx - sign)
        me, t = len(arrivals), end + 300
        arrivals.append((t, me, (part, axis, sign, dz, dx, extent), cause))
        steps, half = abs(dz if axis == "z" else dx), length[axis] // 2
        if extent == "full":
            push(t, me, (part, axis, sign, dz, dx, "full" if steps < half - 1 else "half"))
        if axis == axes[part][0]:
            key = (part, dz % NZ, dx % NX)
            if extent == "full" or key in met:
                starts(t, me, part, axes[part][1], dz, dx)
            met[key] = me
    return sorted(arrivals)


ORDER = plan()
PLACE = {arrival[1]: i for i, arrival in enumerate(ORDER)}
FOLLOW = {}
for i, arrival in enumerate(ORDER):
    FOLLOW.setdefault(None if arrival[3] is None else PLACE[arrival[3]], []).append(i)
for followers in FOLLOW.values():
    followers.sort(key=lambda i: ORDER[i][1])
WHOLE = {}
for i, arrival in enumerate(ORDER):
    WHOLE[arrival[2][0], arrival[2][3] % NZ] = i
COMPLETE = {}
for key, i in WHOLE.items():
    COMPLETE.setdefault(i, []).append(key)


def banded(rows, cols, shift=0):
    i = lax.broadcasted_iota(I32, (rows, cols), 0) + shift
    j = lax.broadcasted_iota(I32, (rows, cols), 1)
    return spread_values(jnp.abs(i - j))


def spread_values(spread):
    coeffs = np.array([-49.0 / 18.0, 1.5, -0.15, 1.0 / 90.0], np.float32)
    coeffs = -0.5 * coeffs.astype(BF16).astype(np.float32)
    out = jnp.zeros(spread.shape, F32)
    for k in range(4):
        out = jnp.where(spread == k, float(coeffs[k]), out)
    return out.astype(BF16)


def two_bands():
    i = lax.broadcasted_iota(I32, (2 * COLS, 2 * COLS), 0)
    j = lax.broadcasted_iota(I32, (2 * COLS, 2 * COLS), 1)
    return spread_values(jnp.where(i // COLS == j // COLS, jnp.abs(i - j), 9))


def cut(pot, region, block, first, rows):
    tile, shift = lax.shift_right_logical(block, 3) + first // 16, 2 * (block & 7)
    chip, core = lax.shift_right_logical(region, 1), region & 1
    parts = []
    for k in range(rows // 16 + 1):
        raw = pot[chip, core, lax.min(tile + k, REG_ROWS // 16 - 1)].astype(F32)
        parts += [raw[0:8], raw[8:16]]
    odd = shift >= 8
    parts = [jnp.where(odd, parts[k + 1], parts[k]) for k in range(rows // 8 + 1)]
    within = shift & 7
    parts = [pltpu.roll(part, (8 - within) & 7, axis=0) for part in parts]
    stays = lax.broadcasted_iota(I32, (8, COLS), 0) < 8 - within
    return jnp.concatenate([jnp.where(stays, parts[k], parts[k + 1]) for k in range(rows // 8)], axis=0)


def pair_of(x_ref, i):
    return [x_ref[2 * i], x_ref[2 * i + 1]]


def filtered(xs, skip, rows, krow, kcol):
    x = jnp.concatenate(xs, axis=1)
    rows_part = jnp.dot(krow[...], x, preferred_element_type=F32)
    return rows_part + jnp.dot(x[skip : skip + rows], kcol[...], preferred_element_type=F32)


def prepare(x_ref, rows, krow, kcol, kinetic, x_to, first, count):
    def body(i, _):
        xs = pair_of(x_ref, i)
        both = filtered(xs, 0, rows, krow, kcol)
        for h in range(2):
            kinetic[2 * i + h] = both[:, COLS * h : COLS * (h + 1)]
            x_to[pl.ds(2 * i + h, rows, stride=PITCH), :] = xs[h].astype(F32)
        return 0

    lax.fori_loop(first, first + count, body, 0, unroll=2)


def finish(x_ref, rows, pot, meta, line, kinetic, out, a_to):
    def body(f, _):
        local = cut(pot, meta[0, line, 0, f], meta[1, line, 0, f], 0, rows) * x_ref[f].astype(F32)
        a = (kinetic[f] + local).astype(BF16)
        out[f] = a
        a_to[pl.ds(f, rows, stride=PITCH), :] = a.astype(F32)
        return 0

    lax.fori_loop(0, COUNT, body, 0, unroll=2)


def apply_block(x_ref, first_in, rows_in, first_out, rows_out, krow, kcol, pot, meta, line, x_to, a_to):
    skip = first_out - first_in

    def body(i, _):
        xs = pair_of(x_ref, i)
        kinetic = filtered(xs, skip, rows_out, krow, kcol)
        for h in range(2):
            f = 2 * i + h
            window = cut(pot, meta[0, line, 0, f], meta[1, line, 0, f], first_out, rows_out)
            values = xs[h].astype(F32)
            a = kinetic[:, COLS * h : COLS * (h + 1)] + window * values[skip : skip + rows_out]
            a_to[pl.ds(f, rows_out, stride=PITCH), :] = a.astype(BF16).astype(F32)
            x_to[pl.ds(f, rows_in, stride=PITCH), :] = values
        return 0

    lax.fori_loop(0, COUNT // 2, body, 0, unroll=8)


def gram(first, last, lhs, rhs):
    def rows(refs, r):
        return jnp.concatenate(
            [
                jnp.concatenate(
                    [ref[pl.ds(pl.multiple_of((r + k - start) * PITCH, 8), COUNT), :].astype(BF16) for k in range(16)],
                    axis=1,
                )
                for ref, start in refs
            ],
            axis=0,
        )

    def body(i, total):
        r = first + 16 * i
        return total + lax.dot_general(
            rows(lhs, r), rows(rhs, r), (((1,), (1,)), ((), ())), preferred_element_type=F32
        )

    total = jnp.zeros((COUNT * len(lhs), COUNT * len(rhs)), F32)
    return lax.fori_loop(0, (last - first) // 16, body, total, unroll=4)


def lane_pick(x, lanes):
    return jnp.take_along_axis(x, lanes, axis=1, mode="promise_in_bounds")


def kernel(
    tiles_hbm, own_pot, region, block, pairs,
    applied_hbm, table, table_after, wanted,
    pot, tiles, prev, after, applied, krow, kcol, kinetic,
    t_rows, a_rows, tp_rows, ap_rows, tn_rows, an_rows,
    meta_v, meta, to_prev, to_next, from_prev, from_next,
    relay,
    send, recv, sib_send, sib_recv, halo_send, halo_recv, relay_send, relay_recv, small_send, small_recv, local_sem,
):
    g, y = lax.axis_index("grid"), lax.axis_index("atoms")
    z, x, c = g // 8, (g // 2) % 4, g % 2

    def chip(dz, dx):
        return ((z + dz + NZ) % NZ) * NX + (x + dx + NX) % NX

    def at(position):
        position = (position + DEVICES) % DEVICES
        return (position // NY, position % NY)

    me = g * NY + y
    near = {("z", s): (chip(s, 0) * 2 + c, y) for s in (1, -1)}
    near.update({("x", s): (chip(0, s) * 2 + c, y) for s in (1, -1)})
    sibling = (g + 1 - 2 * c, y)
    later, earlier = at(me + 1), at(me - 1)
    everyone = [*near.values(), sibling, later, earlier]
    barrier = pltpu.get_barrier_semaphore()
    for device in everyone:
        pl.semaphore_signal(barrier, inc=1, device_id=device, device_id_type=MESH)
    at_low, at_high = y == 0, y == NY - 1
    at_end = jnp.logical_or(at_low, at_high)
    side = 2 * (y // (NY - 1)) - 1
    opposite = (g, NY - 1 - y)
    onward, ward = ((g - side + 64) % 64, y), ((g + side + 64) % 64, y)

    @pl.when(at_end)
    def _():
        for device in (opposite, ward):
            pl.semaphore_signal(barrier, inc=1, device_id=device, device_id_type=MESH)

    def remote(src, dst, s, r, device):
        return pltpu.make_async_remote_copy(src, dst, s, r, device_id=device, device_id_type=MESH)

    tiles_in = pltpu.make_async_copy(tiles_hbm, tiles, local_sem.at[0])
    tiles_in.start()
    pot[chip(0, 0), c] = own_pot[...].astype(BF16).reshape(REG_ROWS // 16, 16, COLS)
    krow[...] = banded(ROWS, ROWS)
    kcol[...] = two_bands()
    @pl.when(at_end)
    def _():
        pl.semaphore_wait(barrier, len(everyone) + 2)

    @pl.when(jnp.logical_not(at_end))
    def _():
        pl.semaphore_wait(barrier, len(everyone))

    halos = [
        remote(region, meta_v.at[0], halo_send.at[2 * CHUNKS], halo_recv.at[2 * CHUNKS], later),
        remote(block, meta_v.at[1], halo_send.at[2 * CHUNKS + 1], halo_recv.at[2 * CHUNKS + 1], later),
        remote(region, meta_v.at[2], halo_send.at[2 * CHUNKS + 2], halo_recv.at[2 * CHUNKS + 2], earlier),
        remote(block, meta_v.at[3], halo_send.at[2 * CHUNKS + 3], halo_recv.at[2 * CHUNKS + 3], earlier),
    ]

    def chunk(k, up):
        some = pl.ds(k * CHUNK, CHUNK)
        if up:
            return remote(
                tiles_hbm.at[some, pl.ds(0, UP)], prev.at[some], halo_send.at[2 * k], halo_recv.at[2 * k], later
            )
        return remote(
            tiles_hbm.at[some, pl.ds(CUT, DOWN)], after.at[some], halo_send.at[2 * k + 1], halo_recv.at[2 * k + 1],
            earlier,
        )

    def slot(k, up):
        return relay.at[k - CHUNKS + RELAYED, :, pl.ds(0, UP if up else DOWN)]

    def detour(k, up):
        some = pl.ds(k * CHUNK, CHUNK)
        src = tiles_hbm.at[some, pl.ds(0, UP) if up else pl.ds(CUT, DOWN)]
        j = k - CHUNKS + RELAYED
        return remote(src, slot(k, up), halo_send.at[2 * k + 1 - up], relay_recv.at[j], opposite)

    def send_on(k, up):
        some = pl.ds(k * CHUNK, CHUNK)
        j = k - CHUNKS + RELAYED
        dst = prev.at[some] if up else after.at[some]
        return remote(slot(k, up), dst, relay_send.at[j], halo_recv.at[2 * k + 1 - up], onward)

    def send_chunk(k):
        if k < CHUNKS - RELAYED:
            chunk(k, 1).start()
            chunk(k, 0).start()
            return
        for up, edge in ((1, at_high), (0, at_low)):

            @pl.when(edge)
            def _():
                detour(k, up).start()

            @pl.when(jnp.logical_not(edge))
            def _():
                chunk(k, up).start()

    def relay_chunk(k):
        for up, edge in ((1, at_low), (0, at_high)):

            @pl.when(edge)
            def _():
                landed(slot(k, up), relay_recv.at[k - CHUNKS + RELAYED])
                send_on(k, up).start()

    def relay_sent(k):
        for up, edge in ((1, at_low), (0, at_high)):

            @pl.when(edge)
            def _():
                send_on(k, up).wait_send()

    def slab(part, dz, dx, sign, extent):
        low, rows = BASE[part], SIZE[part]
        if extent == "half":
            rows //= 2
            low += 0 if sign > 0 else rows
        return pot.at[chip(dz, dx), c, pl.ds(low // 16, rows // 16)]

    def forward(i):
        part, axis, sign, dz, dx, extent = ORDER[i][2]
        dz, dx = (dz + sign, dx) if axis == "z" else (dz, dx + sign)
        src = slab(part, dz, dx, sign, extent)
        return remote(src, src, send.at[i], recv.at[i], near[axis, sign])

    def plane(key, core):
        part, dz = key
        return pot.at[pl.ds(((z + dz) % NZ) * NX, NX), core, pl.ds(BASE[part] // 16, SIZE[part] // 16)]

    def hand_over(key):
        j = "AB".index(key[0]) * NZ + key[1]
        return remote(plane(key, c), plane(key, c), sib_send.at[j], sib_recv.at[j], sibling)

    def landed(ref, sem):
        pltpu.make_async_copy(ref, ref, sem).wait()

    for i in FOLLOW[None]:
        forward(i).start()
    for copy in halos:
        copy.start()
    for k, when in SEND_AT.items():
        if when == 0:
            send_chunk(k)
    own_meta = [
        pltpu.make_async_copy(region, meta.at[0, 0], local_sem.at[1]),
        pltpu.make_async_copy(block, meta.at[1, 0], local_sem.at[2]),
    ]
    for copy in own_meta:
        copy.start()
    handed = []
    done = 0
    for i in range(len(ORDER)):
        part, axis, sign, dz, dx, extent = ORDER[i][2]
        landed(slab(part, dz, dx, sign, extent), recv.at[i])
        for j in FOLLOW.get(i, []):
            forward(j).start()
        for key in COMPLETE.get(i, []):
            hand_over(key).start()
            handed.append(key)
        for k, when in SEND_AT.items():
            if when == i + 1:
                send_chunk(k)
        for k, when in RELAY_AT.items():
            if when == i + 1:
                relay_chunk(k)
        if i == 7:
            tiles_in.wait()
        if i >= 8 and i % 2 == 0 and done < COUNT // 2:
            prepare(tiles, ROWS, krow, kcol, kinetic, t_rows, done, 2)
            done += 2
    for key in handed:
        landed(plane(key, 1 - c), sib_recv.at["AB".index(key[0]) * NZ + key[1]])
    for copy in own_meta:
        copy.wait()
    finish(tiles, ROWS, pot, meta, 0, kinetic, applied, a_rows)
    out = pltpu.make_async_copy(applied, applied_hbm, local_sem.at[3])
    out.start()
    for copy in halos:
        copy.wait()
    for k in range(CHUNKS):
        chunk(k, 1).wait()
        chunk(k, 0).wait()
    metas = [pltpu.make_async_copy(meta_v.at[k], meta.at[k % 2, 1 + k // 2], local_sem.at[4 + k]) for k in range(4)]
    for copy in metas:
        copy.start()
    for copy in metas:
        copy.wait()
    apply_block(
        prev, 0, UP, 0, CUT, krow.at[0:CUT, 0:UP], kcol, pot, meta, 1, tp_rows, ap_rows
    )
    apply_block(
        after, CUT, DOWN, UP, ROWS - UP, krow.at[UP:ROWS, CUT:ROWS], kcol, pot, meta, 2,
        tn_rows, an_rows,
    )
    own = [(t_rows, 0), (a_rows, 0)]
    low = gram(0, CUT, own, [(t_rows, 0), (tp_rows, 0), (ap_rows, 0)])
    mid = gram(CUT, UP, own, [(t_rows, 0), (tp_rows, 0), (tn_rows, CUT)])
    high = gram(UP, ROWS, own, [(t_rows, 0), (tn_rows, CUT), (an_rows, UP)])
    to_prev[...] = low[0:COUNT, COUNT:]
    to_next[...] = high[0:COUNT, COUNT:]
    to_prev[:, 0:COUNT] = low[0:COUNT, COUNT : 2 * COUNT] + mid[0:COUNT, COUNT : 2 * COUNT]
    results = [
        remote(to_prev, from_next, small_send.at[0], small_recv.at[0], earlier),
        remote(to_next, from_prev, small_send.at[1], small_recv.at[1], later),
    ]
    for copy in results:
        copy.start()
    scale = float(ROWS * COLS) ** -0.5
    one, two, three = slice(0, COUNT), slice(COUNT, 2 * COUNT), slice(2 * COUNT, 3 * COUNT)
    table[:, two] = (low[:, one] + mid[:, one] + high[:, one]) * scale
    lanes = lax.broadcasted_iota(I32, (ATOMS, COLS), 1)
    wide = jnp.concatenate([pairs[...]] * (COLS // PAIRS), axis=1)
    first = (me - 1) * ATOMS
    for k in range(SPA):
        partner = lane_pick(wide, lanes // 16 + 8 * k)
        column = ((partner - first + 2 * DEVICES * ATOMS) % (DEVICES * ATOMS)) * SPA + lanes % SPA
        wanted[:, k * COLS : (k + 1) * COLS] = column
    for copy in results:
        copy.wait()
    table[:, one] = (low[:, two] + mid[:, two] + from_prev[...].T) * scale
    table_after[...] = jnp.zeros_like(table_after)
    table_after[0:COUNT, one] = (high[0:COUNT, two] + from_next[...].T[0:COUNT]) * scale
    table_after[COUNT : 2 * COUNT, one] = (
        high[COUNT : 2 * COUNT, two] + mid[COUNT : 2 * COUNT, three] + from_next[...].T[COUNT : 2 * COUNT]
    ) * scale
    for i in range(len(ORDER)):
        forward(i).wait_send()
    for key in handed:
        hand_over(key).wait_send()
    for k in RELAY_AT:
        relay_sent(k)
    out.wait()


PIECES = 8


def pick(applied_in, table, table_after, wanted, applied, margin, hamiltonian, held, sem):
    some = COUNT // PIECES
    pieces = [pl.ds(k * some, some) for k in range(PIECES)]
    inward = [pltpu.make_async_copy(applied_in.at[at], held.at[at], sem.at[0, k]) for k, at in enumerate(pieces)]
    outward = [pltpu.make_async_copy(held.at[at], applied.at[at], sem.at[1, k]) for k, at in enumerate(pieces)]
    for copy in inward:
        copy.start()
    for k in range(PIECES):
        inward[k].wait()
        outward[k].start()
    lanes = lax.broadcasted_iota(I32, (ATOMS, COLS), 1)
    for k, target in ((0, margin), (1, hamiltonian)):
        for q in range(SPA):
            total = jnp.zeros((ATOMS, COLS), F32)
            for s in range(SPA):
                rows = pl.ds(k * COUNT + s, ATOMS, stride=SPA)
                left, right = table[rows, :], table_after[rows, :]
                column = wanted[:, q * COLS : (q + 1) * COLS]
                inside = column % COLS
                value = jnp.where(column < COLS, lane_pick(left, inside), lane_pick(right, inside))
                total = jnp.where((lanes // SPA) % SPA == s, value, total)
            target[:, q * COLS : (q + 1) * COLS] = total
    for copy in outward:
        copy.wait()


def shards(support_tiles, potential, tile_region, tile_block, pair_atoms):
    vmem, hbm = pl.BlockSpec(memory_space=pltpu.VMEM), pl.BlockSpec(memory_space=pl.ANY)
    dma = pltpu.SemaphoreType.DMA
    messages = len(ORDER)
    served = pl.pallas_call(
        kernel,
        out_shape=(
            jax.ShapeDtypeStruct((COUNT, ROWS, COLS), BF16),
            jax.ShapeDtypeStruct((2 * COUNT, COLS), F32),
            jax.ShapeDtypeStruct((2 * COUNT, COLS), F32),
            jax.ShapeDtypeStruct((ATOMS, PAIRS * SPA * SPA), I32),
        ),
        in_specs=[hbm, vmem, vmem, vmem, vmem],
        out_specs=(hbm, vmem, vmem, vmem),
        scratch_shapes=[
            pltpu.VMEM((NZ * NX, 2, REG_ROWS // 16, 16, COLS), BF16),
            pltpu.VMEM((COUNT, ROWS, COLS), BF16),
            pltpu.VMEM((COUNT, UP, COLS), BF16),
            pltpu.VMEM((COUNT, DOWN, COLS), BF16),
            pltpu.VMEM((COUNT, ROWS, COLS), BF16),
            pltpu.VMEM((ROWS, ROWS), BF16),
            pltpu.VMEM((2 * COLS, 2 * COLS), BF16),
            pltpu.VMEM((COUNT, ROWS, COLS), F32),
            *[pltpu.VMEM((rows * PITCH, COLS), F32) for rows in (ROWS, ROWS, UP, CUT, DOWN, ROWS - UP)],
            pltpu.VMEM((4, 1, COUNT), I32),
            pltpu.SMEM((2, 3, 1, COUNT), I32),
            *[pltpu.VMEM((COUNT, 2 * COUNT), F32) for _ in range(4)],
            pltpu.VMEM((RELAYED, CHUNK, UP, COLS), BF16),
            dma((messages,)), dma((messages,)), dma((2 * NZ,)), dma((2 * NZ,)),
            dma((2 * CHUNKS + 4,)), dma((2 * CHUNKS + 4,)), dma((RELAYED,)), dma((RELAYED,)), dma((2,)), dma((2,)), dma((8,)),
        ],
        compiler_params=pltpu.CompilerParams(
            collective_id=0, has_side_effects=True, vmem_limit_bytes=60 * 2**20
        ),
    )(
        support_tiles,
        potential.reshape(REG_ROWS, COLS),
        tile_region.reshape(1, COUNT),
        tile_block.reshape(1, COUNT),
        pair_atoms,
    )
    blocks = jax.ShapeDtypeStruct((ATOMS, PAIRS * SPA * SPA), F32)
    return pl.pallas_call(
        pick,
        out_shape=(jax.ShapeDtypeStruct((COUNT, ROWS, COLS), BF16), blocks, blocks),
        in_specs=[hbm, vmem, vmem, vmem],
        out_specs=(hbm, vmem, vmem),
        scratch_shapes=[pltpu.VMEM((COUNT, ROWS, COLS), BF16), dma((2, PIECES))],
        compiler_params=pltpu.CompilerParams(vmem_limit_bytes=60 * 2**20),
    )(*served)


def solution(mesh):
    placed = P(("grid", "atoms"))
    return jax.shard_map(
        shards,
        mesh=mesh,
        in_specs=(placed, P("grid"), placed, placed, placed),
        out_specs=(placed, placed, placed),
        check_vma=False,
    )
```
